256 devices in a mesh: layer: 4 (over z_lo, core), latent: 64 (over x, z_hi, y).
Axes of the slice: x: 4, y: 4, z: 8 (z_hi: 4, z_lo: 2; z = z_hi * 2 + z_lo), core: 2. Of those that a mesh axis runs over, the one named last changes fastest.
Arguments:
- acts: bfloat16 [4, 512, 2048], P('layer', None, 'latent'), may hold values from -6 to 6
- w_enc: bfloat16 [4, 2048, 32768], P('layer', None, 'latent'), may hold values from -0.0625 to 0.0625
- b_enc: float32 [32768], P('latent'), may hold values from -3 to 3
- w_dec: bfloat16 [4, 32768, 2048], P('layer', 'latent'), may hold values from -0.09375 to 0.09375
- b_dec: bfloat16 [4, 2048], P('layer', 'latent'), may hold values from -3 to 3
Outputs:
- grad_enc: bfloat16 [4, 2048, 32768], P('layer', None, 'latent')
- grad_dec: bfloat16 [4, 32768, 2048], P('layer', 'latent')
- grad_benc: float32 [32768], P('latent')
- grad_bdec: float32 [4, 2048], P('layer', 'latent')
The draws below stay inside these ranges and needn't reach their ends.
All inputs are finite; a program needn't handle non-finite values.
Results may differ from the reference program's by a relative error of at most 0.014.
Values may be sent and summed in bfloat16 or wider, within the bound.
No kernel may reach another device: no remote copies, remote signals or barrier semaphores. Data moves between devices by JAX's collectives and lax.ppermute only.
A program may use at most 64 MiB of HBM per device.

```python
import jax
import jax.numpy as jnp

D = 4096
LAYERS = 2
TOK = 512
LATENTS = 32768


def with_spikes(entries, rng, source, target, shards_of, factor):
    def block_of(position):
        return (jnp.arange(entries.shape[position]) // (entries.shape[position] // shards_of)).reshape((-1,) + (1,) * (entries.ndim - 1 - position))

    near = jax.random.permutation(rng, shards_of)[block_of(target)]
    second = (block_of(target) + shards_of // 2) % shards_of
    return jnp.where((block_of(source) == near) | (block_of(source) == second), factor * entries, entries)


def levels(key, dims, shards, low, top_value):
    factor_of, own = 1.0, jax.random.fold_in(key, 6)
    for axis_at, blocks in shards:
        heights = jnp.exp(jax.random.uniform(jax.random.fold_in(own, axis_at), (blocks,), jnp.float32, low / len(shards), top_value / len(shards)))
        factor_of = factor_of * jnp.repeat(heights, dims[axis_at] // blocks).reshape([-1 if axis == axis_at else 1 for axis in range(len(dims))])
    return factor_of


def centred(stream_key, shape, width, reach, shards=(), kind=jnp.bfloat16):
    result = jax.random.normal(stream_key, shape, jnp.float32) * width
    if len(shards) > 0:
        result = levels(stream_key, shape, shards, -0.22, 0.18) * result
    return jnp.clip(result, min=-reach, max=reach).astype(kind)


def bell_draw_with(stream_key, extent, deviation, bound, split, heavy, kind=jnp.bfloat16):
    entries = deviation * jax.random.normal(stream_key, extent, jnp.float32)
    if split:
        entries = entries * levels(stream_key, extent, split, -0.22, 0.18)
    return jnp.clip(with_spikes(entries, jax.random.fold_in(stream_key, 3), *heavy), -bound, bound).astype(kind)


def setup_inputs(seed: int = 0) -> dict:
    seeds = jax.random.split(jax.random.key(seed), 6)
    return {
        "acts": centred(seeds[0], (2 * LAYERS, TOK, D // 2), 1.0, 6.0, ((0, 4), (2, 64))),
        "w_enc": centred(seeds[1], (2 * LAYERS, D // 2, LATENTS), (LAYERS * D) ** -0.5, 0.0625, ((0, 4), (2, 64))),
        "b_enc": centred(seeds[2], (LATENTS,), 0.5, 3.0, ((0, 64),), jnp.float32),
        "w_dec": bell_draw_with(seeds[3], (2 * LAYERS, LATENTS, D // 2), LATENTS ** -0.5, 0.09375, ((0, 4), (1, 64)), (1, 2, 64, 4.0)),
        "b_dec": centred(seeds[4], (2 * LAYERS, D // 2), 0.5, 3.0, ((0, 4), (1, 64))),
    }


def reference(acts, w_enc, b_enc, w_dec, b_dec):
    half = D // 2
    full_acts = [jnp.concatenate([acts[2 * i], acts[2 * i + 1]], axis=1) for i in range(LAYERS)]
    full_enc = [jnp.concatenate([w_enc[2 * i], w_enc[2 * i + 1]], axis=0) for i in range(LAYERS)]
    full_dec = [jnp.concatenate([w_dec[2 * i], w_dec[2 * i + 1]], axis=1) for i in range(LAYERS)]
    full_bias = [jnp.concatenate([b_dec[2 * i], b_dec[2 * i + 1]], axis=0) for i in range(LAYERS)]
    pre = jnp.zeros((TOK, LATENTS), jnp.float32) + b_enc[None, :].astype(jnp.float32)
    for layer_idx in range(LAYERS):
        pre = pre + jnp.dot(full_acts[layer_idx], full_enc[layer_idx], preferred_element_type=jnp.float32)
    feat = (jax.nn.softplus(4.0 * pre) / 4.0).astype(jnp.bfloat16)
    scale = TOK ** -0.5
    grad_feat = jnp.zeros((TOK, LATENTS), jnp.float32)
    dec_list = []
    bdec_list = []
    for layer_idx in range(LAYERS):
        recon = jnp.dot(feat, full_dec[layer_idx], preferred_element_type=jnp.float32)
        err = (recon + full_bias[layer_idx][None, :].astype(jnp.float32) - full_acts[layer_idx].astype(jnp.float32)).astype(jnp.bfloat16)
        bias_grad = scale * jnp.sum(err.astype(jnp.float32), axis=0)
        bdec_list.append(bias_grad[:half])
        bdec_list.append(bias_grad[half:])
        dec_grad = (scale * jnp.dot(feat.T, err, preferred_element_type=jnp.float32)).astype(jnp.bfloat16)
        dec_list.append(dec_grad[:, :half])
        dec_list.append(dec_grad[:, half:])
        grad_feat = grad_feat + jnp.dot(err, full_dec[layer_idx].T, preferred_element_type=jnp.float32)
    grad_feat = scale * grad_feat
    grad_pre = grad_feat * jax.nn.sigmoid(4.0 * pre)
    grad_benc = jnp.sum(grad_pre, axis=0)
    grad_pre_b = grad_pre.astype(jnp.bfloat16)
    enc_list = []
    for layer_idx in range(LAYERS):
        enc_grad = jnp.dot(full_acts[layer_idx].T, grad_pre_b, preferred_element_type=jnp.float32).astype(jnp.bfloat16)
        enc_list.append(enc_grad[:half])
        enc_list.append(enc_grad[half:])
    return jnp.stack(enc_list), jnp.stack(dec_list), grad_benc, jnp.stack(bdec_list)
```

```python
import jax
import jax.numpy as jnp
import numpy as np
from jax import lax
from jax.experimental import pallas as pl
from jax.experimental.pallas import tpu as pltpu
from jax.sharding import Mesh
from jax.sharding import PartitionSpec as P

AXES = ("z_lo", "core", "x", "z_hi", "y")
LATENT = ("x", "z_hi", "y")
PLANE = ("core", "x", "y")
ORDER = (2, 1, 3)
BLOCK = 32

VMEM = pl.BlockSpec(memory_space=pltpu.VMEM)
SMEM = pl.BlockSpec(memory_space=pltpu.SMEM)
PARAMS = pltpu.CompilerParams(vmem_limit_bytes=32 * 1024 * 1024)


def other_core(x):
    return lax.ppermute(x, "core", [(0, 1), (1, 0)])


def other_layer(x):
    return lax.ppermute(x, "z_lo", [(0, 1), (1, 0)])


def along_z(x, k):
    return lax.ppermute(x, "z_hi", [(i, i ^ k) for i in range(4)])


def in_plane(x, k, x_core):
    pairs = []
    for c in range(2):
        for i in range(4):
            for j in range(4):
                a, b = (i ^ k, j) if c == x_core else (i, j ^ k)
                pairs.append((c * 16 + i * 4 + j, c * 16 + a * 4 + b))
    return lax.ppermute(x, PLANE, pairs)


def first(x, k):
    return in_plane(x, k, 0)


def second(x, k):
    return in_plane(x, k, 1)


def received(pieces, send):
    got = {k: send(pieces[k], k) for k in ORDER}
    return [pieces[0], got[1], got[2], got[3]]


def gathered(x):
    for send in (along_z, first):
        x = jnp.concatenate(received([x] * 4, send), axis=0)
    return received([x] * 4, second)


def scattered(pieces):
    total = sum(p.astype(jnp.float32) for p in received(pieces, second))
    for send in (first, along_z):
        pieces = jnp.split(total.astype(jnp.bfloat16), 4, axis=0)
        total = sum(p.astype(jnp.float32) for p in received(pieces, send))
    return total


def block_rows():
    c = lax.axis_index("core")
    x, z, y = (lax.axis_index(a) for a in LATENT)
    k = np.arange(64)
    far, near, up = k // 16, (k // 4) % 4, k % 4
    bx = jnp.where(c == 0, near ^ x, far ^ x)
    by = jnp.where(c == 0, far ^ y, near ^ y)
    return (BLOCK * (bx * 16 + (up ^ z) * 4 + by)).astype(jnp.int32)


def assemble(rows, pieces, own, other):
    for k in range(64):
        at = pl.ds(pl.multiple_of(rows[k], BLOCK), BLOCK)
        piece, src = pieces[k // 16], (k % 16) * 2 * BLOCK
        own[at, :] = piece[src : src + BLOCK, :]
        other[at, :] = piece[src + BLOCK : src + 2 * BLOCK, :]


def gathered_dot_kernel(rows, p0, p1, p2, p3, w_own, w_other, own, other, out):
    assemble(rows, (p0, p1, p2, p3), own, other)
    out[...] = (
        jnp.dot(w_own[...], own[...], preferred_element_type=jnp.float32)
        + jnp.dot(w_other[...], other[...], preferred_element_type=jnp.float32)
    ).astype(out.dtype)


def gathered_dot(rows, pieces, w_own, w_other):
    n, depth = w_own.shape
    tokens = pieces[0].shape[1]
    whole = jax.ShapeDtypeStruct((depth, tokens), jnp.bfloat16)
    return pl.pallas_call(
        gathered_dot_kernel,
        out_shape=(whole, whole, jax.ShapeDtypeStruct((n, tokens), jnp.bfloat16)),
        in_specs=[SMEM] + [VMEM] * 6,
        out_specs=(VMEM,) * 3,
        compiler_params=PARAMS,
        cost_estimate=pl.CostEstimate(
            flops=4 * n * depth * tokens, bytes_accessed=8 << 20, transcendentals=0
        ),
    )(rows, *pieces, w_own, w_other)


def blocked_dot_kernel(rows, w_own, w_other, feat, p0, p1, p2, p3, own, other):
    own[...] = jnp.dot(w_own[...], feat[...], preferred_element_type=jnp.float32).astype(own.dtype)
    other[...] = jnp.dot(w_other[...], feat[...], preferred_element_type=jnp.float32).astype(
        own.dtype
    )
    pieces = (p0, p1, p2, p3)
    for k in range(64):
        at = pl.ds(pl.multiple_of(rows[k], BLOCK), BLOCK)
        piece, dst = pieces[k // 16], (k % 16) * 2 * BLOCK
        piece[dst : dst + BLOCK, :] = own[at, :]
        piece[dst + BLOCK : dst + 2 * BLOCK, :] = other[at, :]


def blocked_dot(rows, w_own, w_other, feat):
    width, n = w_own.shape
    tokens = feat.shape[1]
    piece = jax.ShapeDtypeStruct((width // 2, tokens), jnp.bfloat16)
    return pl.pallas_call(
        blocked_dot_kernel,
        out_shape=(piece,) * 4,
        in_specs=[SMEM] + [VMEM] * 3,
        out_specs=(VMEM,) * 4,
        scratch_shapes=[pltpu.VMEM((width, tokens), jnp.bfloat16)] * 2,
        compiler_params=PARAMS,
        cost_estimate=pl.CostEstimate(
            flops=4 * n * width * tokens, bytes_accessed=7 << 20, transcendentals=0
        ),
    )(rows, w_own, w_other, feat)


def outer_kernel(scale, a0, b0, a1, b1, out):
    dims = (((1,), (1,)), ((), ()))
    out[...] = (
        scale
        * (
            lax.dot_general(a0[...], b0[...], dims, preferred_element_type=jnp.float32)
            + lax.dot_general(a1[...], b1[...], dims, preferred_element_type=jnp.float32)
        )
    ).astype(out.dtype)


def outer(a0, b0, a1, b1, scale):
    m, tokens = a0.shape
    n = b0.shape[0]
    tile = m // 4

    def kernel(*refs):
        outer_kernel(scale, *refs)

    rows = pl.BlockSpec((tile, tokens), lambda i: (i, 0))
    whole = pl.BlockSpec((n, tokens), lambda i: (0, 0))
    return pl.pallas_call(
        kernel,
        out_shape=jax.ShapeDtypeStruct((m, n), jnp.bfloat16),
        grid=(4,),
        in_specs=[rows, whole, rows, whole],
        out_specs=pl.BlockSpec((tile, n), lambda i: (i, 0)),
        compiler_params=PARAMS,
        cost_estimate=pl.CostEstimate(
            flops=4 * m * n * tokens, bytes_accessed=5 << 20, transcendentals=0
        ),
    )(a0, b0, a1, b1)


def body(acts, w_enc, b_enc, w_dec, b_dec):
    tokens_all = acts.shape[1]
    half = tokens_all // 2
    scale = tokens_all ** (-0.5)
    core = lax.axis_index("core")
    rows = block_rows()

    local = acts[0].T
    bias = jnp.broadcast_to(b_dec[0][:, None], (local.shape[0], 128))
    mine = lax.dynamic_slice_in_dim(local, core * half, half, 1)
    theirs = lax.dynamic_slice_in_dim(local, (1 - core) * half, half, 1)
    swapped = other_core(jnp.concatenate([theirs, bias], axis=1))
    start = jnp.concatenate([mine, swapped[:, :half]], axis=0)
    bias_both = jnp.concatenate([bias[:, :1], swapped[:, half : half + 1]], axis=0)

    enc_t = w_enc[0].T
    dec = w_dec[0]
    dec_t = dec.T
    enc_t, dec, dec_t = lax.optimization_barrier((enc_t, dec, dec_t))
    enc_t_other, dec_t_other, dec_other = (other_core(w) for w in (enc_t, dec_t, dec))

    acts_own, acts_other, part = gathered_dot(rows, gathered(start), enc_t, enc_t_other)
    part_b = other_layer(part)
    pre = part.astype(jnp.float32) + part_b.astype(jnp.float32) + b_enc[:, None]
    feat = (jax.nn.softplus(4.0 * pre) / 4.0).astype(jnp.bfloat16)
    feat_b = other_core(feat)
    acts_b = other_core(acts_other)

    recon = scattered(blocked_dot(rows, dec_t, dec_t_other, feat))
    err = (recon + bias_both.astype(jnp.float32) - start.astype(jnp.float32)).astype(jnp.bfloat16)
    sums = jnp.sum(err.astype(jnp.float32), axis=1)
    width = sums.shape[0] // 2
    grad_bdec = scale * (sums[:width] + other_core(sums[width:]))

    err_own, err_other, term = gathered_dot(rows, gathered(err), dec, dec_other)
    term_b = other_layer(term)
    err_b = other_core(err_other)
    grad_dec = outer(feat, err_own, feat_b, err_b, scale)

    grad_feat = scale * (term.astype(jnp.float32) + term_b.astype(jnp.float32))
    grad_pre = grad_feat * jax.nn.sigmoid(4.0 * pre)
    grad_pre_b = grad_pre.astype(jnp.bfloat16)
    grad_pre_o = other_core(grad_pre_b)
    part_benc = jnp.sum(grad_pre, axis=1)
    grad_benc = part_benc + other_core(part_benc)
    grad_enc = outer(acts_own, grad_pre_b, acts_b, grad_pre_o, 1.0)
    return (grad_enc[None], grad_dec[None], grad_benc, grad_bdec[None])


def solution(mesh):
    finer = Mesh(mesh.devices.reshape(2, 2, 4, 4, 4), AXES)
    layer = ("z_lo", "core")
    return jax.shard_map(
        body,
        mesh=finer,
        in_specs=(
            P(layer, None, LATENT),
            P(layer, None, LATENT),
            P(LATENT),
            P(layer, LATENT, None),
            P(layer, LATENT),
        ),
        out_specs=(
            P(layer, None, LATENT),
            P(layer, LATENT, None),
            P(LATENT),
            P(layer, LATENT),
        ),
        check_vma=False,
    )
```

```python
import jax
import jax.numpy as jnp
import numpy as np
from jax import lax
from jax.experimental import pallas as pl
from jax.experimental.pallas import tpu as pltpu
from jax.sharding import Mesh
from jax.sharding import PartitionSpec as P

AXES = ("z_lo", "core", "x", "z_hi", "y")
LATENT = ("x", "z_hi", "y")
PLANE = ("core", "x", "y")
ORDER = (2, 1, 3)
BLOCK = 32

VMEM = pl.BlockSpec(memory_space=pltpu.VMEM)
FAR = pl.BlockSpec(memory_space=pltpu.HBM)
SMEM = pl.BlockSpec(memory_space=pltpu.SMEM)
PARAMS = pltpu.CompilerParams(vmem_limit_bytes=16 * 1024 * 1024)


def other_core(x):
    return lax.ppermute(x, "core", [(0, 1), (1, 0)])


def other_layer(x):
    return lax.ppermute(x, "z_lo", [(0, 1), (1, 0)])


def along_z(x, k):
    return lax.ppermute(x, "z_hi", [(i, i ^ k) for i in range(4)])


def in_plane(x, k, x_core):
    pairs = []
    for c in range(2):
        for i in range(4):
            for j in range(4):
                a, b = (i ^ k, j) if c == x_core else (i, j ^ k)
                pairs.append((c * 16 + i * 4 + j, c * 16 + a * 4 + b))
    return lax.ppermute(x, PLANE, pairs)


def first(x, k):
    return in_plane(x, k, 0)


def second(x, k):
    return in_plane(x, k, 1)


def received(pieces, send):
    got = {k: send(pieces[k], k) for k in ORDER}
    return [pieces[0], got[1], got[2], got[3]]


def gathered(x, beside=()):
    for send in (along_z, first):
        x = jnp.concatenate(received([x] * 4, send), axis=0)
    x, beside = lax.optimization_barrier((x, beside))
    return received([x] * 4, second), beside


def scattered(pieces):
    total = sum(p.astype(jnp.float32) for p in received(pieces, second))
    for send in (first, along_z):
        pieces = jnp.split(total.astype(jnp.bfloat16), 4, axis=0)
        total = sum(p.astype(jnp.float32) for p in received(pieces, send))
    return total


def block_rows():
    c = lax.axis_index("core")
    x, z, y = (lax.axis_index(a) for a in LATENT)
    k = np.arange(64)
    far, near, up = k // 16, (k // 4) % 4, k % 4
    bx = jnp.where(c == 0, near ^ x, far ^ x)
    by = jnp.where(c == 0, far ^ y, near ^ y)
    return (BLOCK * (bx * 16 + (up ^ z) * 4 + by)).astype(jnp.int32)


def relative_enc_kernel(rows, own, other, out, blocks):
    step = pl.program_id(0)
    for k in range(16):
        at = pl.ds(pl.multiple_of(rows[step * 16 + k], BLOCK), BLOCK)
        blocks[2 * k * BLOCK : (2 * k + 1) * BLOCK, :] = own[at, :]
        blocks[(2 * k + 1) * BLOCK : (2 * k + 2) * BLOCK, :] = other[at, :]
    out[0] = blocks[...].T


def relative_enc(rows, own, other):
    depth, n = own.shape
    whole = pl.BlockSpec((depth, n), lambda i: (0, 0))
    return pl.pallas_call(
        relative_enc_kernel,
        out_shape=jax.ShapeDtypeStruct((4, n, depth // 2), jnp.bfloat16),
        grid=(4,),
        in_specs=[SMEM, whole, whole],
        out_specs=pl.BlockSpec((1, n, depth // 2), lambda i: (i, 0, 0)),
        scratch_shapes=[pltpu.VMEM((depth // 2, n), jnp.bfloat16)],
        compiler_params=PARAMS,
        cost_estimate=pl.CostEstimate(flops=1 << 20, bytes_accessed=16 << 20, transcendentals=0),
    )(rows, own, other)


def relative_dec_kernel(rows, own, other, out, own_t, other_t):
    @pl.when(pl.program_id(0) == 0)
    def _():
        width = own.shape[1]
        for j in range(0, width, 512):
            own_t[j : j + 512, :] = own[:, j : j + 512].T
            other_t[j : j + 512, :] = other[:, j : j + 512].T

    step = pl.program_id(0)
    for k in range(16):
        at = pl.ds(pl.multiple_of(rows[step * 16 + k], BLOCK), BLOCK)
        out[0, 2 * k * BLOCK : (2 * k + 1) * BLOCK, :] = own_t[at, :]
        out[0, (2 * k + 1) * BLOCK : (2 * k + 2) * BLOCK, :] = other_t[at, :]


def relative_dec(rows, own, other):
    n, width = own.shape
    whole = pl.BlockSpec((n, width), lambda i: (0, 0))
    return pl.pallas_call(
        relative_dec_kernel,
        out_shape=jax.ShapeDtypeStruct((4, width // 2, n), jnp.bfloat16),
        grid=(4,),
        in_specs=[SMEM, whole, whole],
        out_specs=pl.BlockSpec((1, width // 2, n), lambda i: (i, 0, 0)),
        scratch_shapes=[pltpu.VMEM((width, n), jnp.bfloat16)] * 2,
        compiler_params=PARAMS,
        cost_estimate=pl.CostEstimate(flops=1 << 20, bytes_accessed=16 << 20, transcendentals=0),
    )(rows, own, other)


def turned_kernel(x, out):
    out[0] = x[0].T


def turned(x):
    m, n = x.shape[1:]
    return pl.pallas_call(
        turned_kernel,
        out_shape=jax.ShapeDtypeStruct((4, n, m), jnp.bfloat16),
        grid=(4,),
        in_specs=[pl.BlockSpec((1, m, n), lambda i: (i, 0, 0))],
        out_specs=pl.BlockSpec((1, n, m), lambda i: (i, 0, 0)),
        compiler_params=PARAMS,
        cost_estimate=pl.CostEstimate(flops=1 << 20, bytes_accessed=16 << 20, transcendentals=0),
    )(x)


def gathered_dot_kernel(w, p0, p1, p2, p3, out, held, sems):
    copies = [pltpu.make_async_copy(w.at[k], held.at[k], sems.at[k]) for k in range(4)]
    for copy in copies:
        copy.start()
    total = None
    for k, piece in enumerate((p0, p1, p2, p3)):
        copies[k].wait()
        term = jnp.dot(held[k], piece[...], preferred_element_type=jnp.float32)
        total = term if total is None else total + term
    out[...] = total.astype(out.dtype)


def gathered_dot(w, pieces):
    _, n, depth = w.shape
    tokens = pieces[0].shape[1]
    return pl.pallas_call(
        gathered_dot_kernel,
        out_shape=jax.ShapeDtypeStruct((n, tokens), jnp.bfloat16),
        in_specs=[FAR] + [VMEM] * 4,
        out_specs=VMEM,
        scratch_shapes=[pltpu.VMEM(w.shape, jnp.bfloat16), pltpu.SemaphoreType.DMA((4,))],
        compiler_params=PARAMS,
        cost_estimate=pl.CostEstimate(
            flops=8 * n * depth * tokens, bytes_accessed=8 << 20, transcendentals=0
        ),
    )(w, *pieces)


def blocked_dot_kernel(w, feat, p0, p1, p2, p3, held, sems):
    order = ((2, p2), (1, p1), (3, p3), (0, p0))
    copies = {k: pltpu.make_async_copy(w.at[k], held.at[k], sems.at[k]) for k, _ in order}
    for k, _ in order:
        copies[k].start()
    for k, piece in order:
        copies[k].wait()
        piece[...] = jnp.dot(held[k], feat[...], preferred_element_type=jnp.float32).astype(
            piece.dtype
        )


def blocked_dot(w, feat):
    _, width, n = w.shape
    tokens = feat.shape[1]
    piece = jax.ShapeDtypeStruct((width, tokens), jnp.bfloat16)
    return pl.pallas_call(
        blocked_dot_kernel,
        out_shape=(piece,) * 4,
        in_specs=[FAR, VMEM],
        out_specs=(VMEM,) * 4,
        scratch_shapes=[pltpu.VMEM(w.shape, jnp.bfloat16), pltpu.SemaphoreType.DMA((4,))],
        compiler_params=PARAMS,
        cost_estimate=pl.CostEstimate(
            flops=8 * n * width * tokens, bytes_accessed=7 << 20, transcendentals=0
        ),
    )(w, feat)


def placed_kernel(rows, p0, p1, p2, p3, own, other):
    for k in range(64):
        at = pl.ds(pl.multiple_of(rows[k], BLOCK), BLOCK)
        piece, src = (p0, p1, p2, p3)[k // 16], (k % 16) * 2 * BLOCK
        own[at, :] = piece[src : src + BLOCK, :]
        other[at, :] = piece[src + BLOCK : src + 2 * BLOCK, :]


def placed(rows, pieces):
    depth, tokens = pieces[0].shape
    whole = jax.ShapeDtypeStruct((2 * depth, tokens), jnp.bfloat16)
    return pl.pallas_call(
        placed_kernel,
        out_shape=(whole, whole),
        in_specs=[SMEM] + [VMEM] * 4,
        out_specs=(VMEM,) * 2,
        compiler_params=PARAMS,
        cost_estimate=pl.CostEstimate(flops=1 << 20, bytes_accessed=4 << 20, transcendentals=0),
    )(rows, *pieces)


def outer_kernel(scale, a0, b0, a1, b1, out):
    dims = (((1,), (1,)), ((), ()))
    out[...] = (
        scale
        * (
            lax.dot_general(a0[...], b0[...], dims, preferred_element_type=jnp.float32)
            + lax.dot_general(a1[...], b1[...], dims, preferred_element_type=jnp.float32)
        )
    ).astype(out.dtype)


def outer(a0, b0, a1, b1, scale):
    m, tokens = a0.shape
    n = b0.shape[0]
    tile = 512

    def kernel(*refs):
        outer_kernel(scale, *refs)

    if m > n:
        left = pl.BlockSpec((tile, tokens), lambda i: (i, 0))
        right = pl.BlockSpec((n, tokens), lambda i: (0, 0))
        out = pl.BlockSpec((tile, n), lambda i: (i, 0))
    else:
        left = pl.BlockSpec((m, tokens), lambda i: (0, 0))
        right = pl.BlockSpec((tile, tokens), lambda i: (i, 0))
        out = pl.BlockSpec((m, tile), lambda i: (0, i))
    return pl.pallas_call(
        kernel,
        out_shape=jax.ShapeDtypeStruct((m, n), jnp.bfloat16),
        grid=(max(m, n) // tile,),
        in_specs=[left, right, left, right],
        out_specs=out,
        compiler_params=PARAMS,
        cost_estimate=pl.CostEstimate(
            flops=40 * m * n * tokens, bytes_accessed=5 << 20, transcendentals=0
        ),
    )(a0, b0, a1, b1)


def body(acts, w_enc, b_enc, w_dec, b_dec):
    tokens_all = acts.shape[1]
    half = tokens_all // 2
    scale = tokens_all ** (-0.5)
    core = lax.axis_index("core")
    rows = block_rows()

    local = acts[0].T
    bias = jnp.broadcast_to(b_dec[0][:, None], (local.shape[0], 128))
    mine = lax.dynamic_slice_in_dim(local, core * half, half, 1)
    theirs = lax.dynamic_slice_in_dim(local, (1 - core) * half, half, 1)
    swapped = other_core(jnp.concatenate([theirs, bias], axis=1))
    start = jnp.concatenate([mine, swapped[:, :half]], axis=0)
    bias_both = jnp.concatenate([bias[:, :1], swapped[:, half : half + 1]], axis=0)

    start, enc, dec = lax.optimization_barrier((start, w_enc[0], w_dec[0]))
    enc_other, dec_other = other_core(enc), other_core(dec)
    acts_p, weights = gathered(start, (enc, enc_other, dec, dec_other))
    enc_r = relative_enc(rows, *weights[:2])
    dec_r = relative_dec(rows, *weights[2:])
    dec_rt = turned(dec_r)

    part = gathered_dot(enc_r, acts_p)
    part, acts_p = lax.optimization_barrier((part, acts_p))
    part_b = other_layer(part)
    acts_own, acts_other = placed(rows, acts_p)
    acts_b = other_core(acts_other)
    part_b, acts_b = lax.optimization_barrier((part_b, acts_b))
    pre = part.astype(jnp.float32) + part_b.astype(jnp.float32) + b_enc[:, None]
    feat = (jax.nn.softplus(4.0 * pre) / 4.0).astype(jnp.bfloat16)

    recon = scattered(blocked_dot(dec_r, feat))
    err = (recon + bias_both.astype(jnp.float32) - start.astype(jnp.float32)).astype(jnp.bfloat16)

    err_p, _ = gathered(err)
    term = gathered_dot(dec_rt, err_p)
    term, err_p, feat, err = lax.optimization_barrier((term, err_p, feat, err))
    term_b = other_layer(term)
    err_own, err_other = placed(rows, err_p)
    err_b, feat_b = other_core(err_other), other_core(feat)
    sums = jnp.sum(err.astype(jnp.float32), axis=1)
    width = sums.shape[0] // 2
    grad_bdec = scale * (sums[:width] + other_core(sums[width:]))
    term_b, err_b, feat_b, grad_bdec = lax.optimization_barrier((term_b, err_b, feat_b, grad_bdec))
    grad_dec = outer(feat, err_own, feat_b, err_b, scale)

    grad_feat = scale * (term.astype(jnp.float32) + term_b.astype(jnp.float32))
    grad_pre = grad_feat * jax.nn.sigmoid(4.0 * pre)
    grad_pre_b = grad_pre.astype(jnp.bfloat16)
    grad_pre_o = other_core(grad_pre_b)
    part_benc = jnp.sum(grad_pre, axis=1)
    grad_benc = part_benc + other_core(part_benc)
    grad_enc = outer(acts_own, grad_pre_b, acts_b, grad_pre_o, 1.0)
    return (grad_enc[None], grad_dec[None], grad_benc, grad_bdec[None])


def solution(mesh):
    finer = Mesh(mesh.devices.reshape(2, 2, 4, 4, 4), AXES)
    layer = ("z_lo", "core")
    return jax.shard_map(
        body,
        mesh=finer,
        in_specs=(
            P(layer, None, LATENT),
            P(layer, None, LATENT),
            P(LATENT),
            P(layer, LATENT, None),
            P(layer, LATENT),
        ),
        out_specs=(
            P(layer, None, LATENT),
            P(layer, LATENT, None),
            P(LATENT),
            P(layer, LATENT),
        ),
        check_vma=False,
    )
```

```python
import functools

import jax
import jax.numpy as jnp
import numpy as np
from jax import lax
from jax.experimental import pallas as pl
from jax.experimental.pallas import tpu as pltpu
from jax.sharding import Mesh
from jax.sharding import PartitionSpec as P

AXES = ("z_lo", "core", "x", "z_hi", "y")
LATENT = ("x", "z_hi", "y")
PLANE = ("core", "x", "y")
ORDER = (2, 1, 3)
BLOCK = 32

VMEM = pl.BlockSpec(memory_space=pltpu.VMEM)
SMEM = pl.BlockSpec(memory_space=pltpu.SMEM)
PARAMS = pltpu.CompilerParams(vmem_limit_bytes=16 * 1024 * 1024)


def other_core(x):
    return lax.ppermute(x, "core", [(0, 1), (1, 0)])


def other_layer(x):
    return lax.ppermute(x, "z_lo", [(0, 1), (1, 0)])


def along_z(x, k):
    return lax.ppermute(x, "z_hi", [(i, i ^ k) for i in range(4)])


def in_plane(x, k, x_core):
    pairs = []
    for c in range(2):
        for i in range(4):
            for j in range(4):
                a, b = (i ^ k, j) if c == x_core else (i, j ^ k)
                pairs.append((c * 16 + i * 4 + j, c * 16 + a * 4 + b))
    return lax.ppermute(x, PLANE, pairs)


def first(x, k):
    return in_plane(x, k, 0)


def second(x, k):
    return in_plane(x, k, 1)


def received(pieces, send):
    got = {k: send(pieces[k], k) for k in ORDER}
    return [pieces[0], got[1], got[2], got[3]]


def gathered(x):
    for k in (1, 2):
        x = jnp.concatenate([x, along_z(x, k)], axis=0)
    x = jnp.concatenate(received([x] * 4, first), axis=0)
    return received([x] * 4, second)


def summed(pieces):
    return sum(p.astype(jnp.float32) for p in pieces)


def scattered(pieces, beside):
    pieces, beside = lax.optimization_barrier((pieces, beside))
    total = summed(received(pieces, second))
    total, swapped = lax.optimization_barrier((total, [other_core(b) for b in beside]))
    total = summed(received(jnp.split(total.astype(jnp.bfloat16), 4, axis=0), first))
    for k in (2, 1):
        kept, sent = jnp.split(total.astype(jnp.bfloat16), 2, axis=0)
        total = summed([kept, along_z(sent, k)])
    return total, swapped


def block_rows():
    c = lax.axis_index("core")
    x, z, y = (lax.axis_index(a) for a in LATENT)
    k = np.arange(64)
    far, near, up = k // 16, (k // 4) % 4, k % 4
    bx = jnp.where(c == 0, near ^ x, far ^ x)
    by = jnp.where(c == 0, far ^ y, near ^ y)
    return (BLOCK * (bx * 16 + (up ^ z) * 4 + by)).astype(jnp.int32)


def relative_enc_kernel(rows, own, other, out, blocks):
    step = pl.program_id(0)
    for k in range(16):
        at = pl.ds(pl.multiple_of(rows[step * 16 + k], BLOCK), BLOCK)
        blocks[2 * k * BLOCK : (2 * k + 1) * BLOCK, :] = own[at, :]
        blocks[(2 * k + 1) * BLOCK : (2 * k + 2) * BLOCK, :] = other[at, :]
    out[0] = blocks[...].T


def relative_enc(rows, own, other):
    depth, n = own.shape
    whole = pl.BlockSpec((depth, n), lambda i: (0, 0))
    return pl.pallas_call(
        relative_enc_kernel,
        out_shape=jax.ShapeDtypeStruct((4, n, depth // 2), jnp.bfloat16),
        grid=(4,),
        in_specs=[SMEM, whole, whole],
        out_specs=pl.BlockSpec((1, n, depth // 2), lambda i: (i, 0, 0)),
        scratch_shapes=[pltpu.VMEM((depth // 2, n), jnp.bfloat16)],
        compiler_params=PARAMS,
        cost_estimate=pl.CostEstimate(flops=1 << 20, bytes_accessed=16 << 20, transcendentals=0),
    )(rows, own, other)


def relative_dec_kernel(rows, own, other, out, own_t, other_t):
    @pl.when(pl.program_id(0) == 0)
    def _():
        width = own.shape[1]
        for j in range(0, width, 512):
            own_t[j : j + 512, :] = own[:, j : j + 512].T
            other_t[j : j + 512, :] = other[:, j : j + 512].T

    step = pl.program_id(0)
    for k in range(16):
        at = pl.ds(pl.multiple_of(rows[step * 16 + k], BLOCK), BLOCK)
        out[0, 2 * k * BLOCK : (2 * k + 1) * BLOCK, :] = own_t[at, :]
        out[0, (2 * k + 1) * BLOCK : (2 * k + 2) * BLOCK, :] = other_t[at, :]


def relative_dec(rows, own, other):
    n, width = own.shape
    whole = pl.BlockSpec((n, width), lambda i: (0, 0))
    return pl.pallas_call(
        relative_dec_kernel,
        out_shape=jax.ShapeDtypeStruct((4, width // 2, n), jnp.bfloat16),
        grid=(4,),
        in_specs=[SMEM, whole, whole],
        out_specs=pl.BlockSpec((1, width // 2, n), lambda i: (i, 0, 0)),
        scratch_shapes=[pltpu.VMEM((width, n), jnp.bfloat16)] * 2,
        compiler_params=PARAMS,
        cost_estimate=pl.CostEstimate(flops=1 << 20, bytes_accessed=16 << 20, transcendentals=0),
    )(rows, own, other)


def turned_kernel(x, out):
    out[0] = x[0].T


def turned(x):
    m, n = x.shape[1:]
    return pl.pallas_call(
        turned_kernel,
        out_shape=jax.ShapeDtypeStruct((4, n, m), jnp.bfloat16),
        grid=(4,),
        in_specs=[pl.BlockSpec((1, m, n), lambda i: (i, 0, 0))],
        out_specs=pl.BlockSpec((1, n, m), lambda i: (i, 0, 0)),
        compiler_params=PARAMS,
        cost_estimate=pl.CostEstimate(flops=1 << 20, bytes_accessed=16 << 20, transcendentals=0),
    )(x)


def gathered_dot_kernel(w, p0, p1, p2, p3, out):
    terms = [
        jnp.dot(w[k], p[...], preferred_element_type=jnp.float32)
        for k, p in enumerate((p0, p1, p2, p3))
    ]
    out[...] = (terms[0] + terms[1] + terms[2] + terms[3]).astype(out.dtype)


def gathered_dot(w, pieces):
    _, n, depth = w.shape
    tokens = pieces[0].shape[1]
    return pl.pallas_call(
        gathered_dot_kernel,
        out_shape=jax.ShapeDtypeStruct((n, tokens), jnp.bfloat16),
        in_specs=[VMEM] * 5,
        out_specs=VMEM,
        compiler_params=PARAMS,
        cost_estimate=pl.CostEstimate(
            flops=8 * n * depth * tokens, bytes_accessed=8 << 20, transcendentals=0
        ),
    )(w, *pieces)


def blocked_dot_kernel(w, feat, *pieces):
    for k, piece in enumerate(pieces):
        piece[...] = jnp.dot(w[k], feat[...], preferred_element_type=jnp.float32).astype(
            piece.dtype
        )


def blocked_dot(w, feat):
    _, width, n = w.shape
    tokens = feat.shape[1]
    piece = jax.ShapeDtypeStruct((width, tokens), jnp.bfloat16)
    return pl.pallas_call(
        blocked_dot_kernel,
        out_shape=(piece,) * 4,
        in_specs=[VMEM] * 2,
        out_specs=(VMEM,) * 4,
        compiler_params=PARAMS,
        cost_estimate=pl.CostEstimate(
            flops=8 * n * width * tokens, bytes_accessed=7 << 20, transcendentals=0
        ),
    )(w, feat)


def placed_kernel(rows, p0, p1, p2, p3, own, other):
    for k in range(64):
        at = pl.ds(pl.multiple_of(rows[k], BLOCK), BLOCK)
        piece, src = (p0, p1, p2, p3)[k // 16], (k % 16) * 2 * BLOCK
        own[at, :] = piece[src : src + BLOCK, :]
        other[at, :] = piece[src + BLOCK : src + 2 * BLOCK, :]


def placed(rows, pieces):
    depth, tokens = pieces[0].shape
    whole = jax.ShapeDtypeStruct((2 * depth, tokens), jnp.bfloat16)
    return pl.pallas_call(
        placed_kernel,
        out_shape=(whole, whole),
        in_specs=[SMEM] + [VMEM] * 4,
        out_specs=(VMEM,) * 2,
        compiler_params=PARAMS,
        cost_estimate=pl.CostEstimate(flops=1 << 20, bytes_accessed=4 << 20, transcendentals=0),
    )(rows, *pieces)


def dot_nt(a, b):
    return lax.dot_general(a, b, (((1,), (1,)), ((), ())), preferred_element_type=jnp.float32)


def outer_dec_kernel(scale, feat, err, feat_b, err_b, out):
    out[...] = (scale * (dot_nt(feat[...], err[...]) + dot_nt(feat_b[...], err_b[...]))).astype(
        out.dtype
    )


def outer_dec(feat, err, feat_b, err_b, scale):
    m, tokens = feat.shape
    n = err.shape[0]
    tile = n // 4
    left = pl.BlockSpec((m, tokens), lambda i: (0, 0))
    right = pl.BlockSpec((tile, tokens), lambda i: (i, 0))
    return pl.pallas_call(
        functools.partial(outer_dec_kernel, scale),
        out_shape=jax.ShapeDtypeStruct((m, n), jnp.bfloat16),
        grid=(4,),
        in_specs=[left, right, left, right],
        out_specs=pl.BlockSpec((m, tile), lambda i: (0, i)),
        compiler_params=PARAMS,
        cost_estimate=pl.CostEstimate(
            flops=40 * m * n * tokens, bytes_accessed=5 << 20, transcendentals=0
        ),
    )(feat, err, feat_b, err_b)


def outer_enc_kernel(acts, grad, grad_b, *rest):
    acts_b, out = rest[:-1], rest[-1]
    own = dot_nt(acts[...], grad[...])
    for j, part in enumerate(acts_b):

        @pl.when(pl.program_id(0) == j)
        def _():
            out[...] = (own + dot_nt(part[...], grad_b[...])).astype(out.dtype)


def outer_enc(acts, grad, acts_b, grad_b):
    m, tokens = acts.shape
    n = grad.shape[0]
    tile = m // len(acts_b)
    rows = pl.BlockSpec((tile, tokens), lambda i: (i, 0))
    return pl.pallas_call(
        outer_enc_kernel,
        out_shape=jax.ShapeDtypeStruct((m, n), jnp.bfloat16),
        grid=(len(acts_b),),
        in_specs=[rows] + [VMEM] * (2 + len(acts_b)),
        out_specs=pl.BlockSpec((tile, n), lambda i: (i, 0)),
        compiler_params=PARAMS,
        cost_estimate=pl.CostEstimate(
            flops=40 * m * n * tokens, bytes_accessed=5 << 20, transcendentals=0
        ),
    )(acts, grad, grad_b, *acts_b)


def body(acts, w_enc, b_enc, w_dec, b_dec):
    tokens_all = acts.shape[1]
    half = tokens_all // 2
    scale = tokens_all ** (-0.5)
    core = lax.axis_index("core")
    rows = block_rows()

    local = acts[0].T
    bias = jnp.broadcast_to(b_dec[0][:, None], (local.shape[0], 128))
    mine = lax.dynamic_slice_in_dim(local, core * half, half, 1)
    theirs = lax.dynamic_slice_in_dim(local, (1 - core) * half, half, 1)
    swapped = other_core(jnp.concatenate([theirs, bias], axis=1))
    start = jnp.concatenate([mine, swapped[:, :half]], axis=0)
    bias_both = jnp.concatenate([bias[:, :1], swapped[:, half : half + 1]], axis=0)

    start, enc, dec = lax.optimization_barrier((start, w_enc[0], w_dec[0]))
    enc_other, dec_other = other_core(enc), other_core(dec)
    enc_r = relative_enc(rows, enc, enc_other)
    dec_r = relative_dec(rows, dec, dec_other)
    acts_p = gathered(start)
    dec_rt = turned(dec_r)

    part = gathered_dot(enc_r, acts_p)
    part, acts_p = lax.optimization_barrier((part, acts_p))
    part_b = other_layer(part)
    acts_own, acts_other = placed(rows, acts_p)
    pre = part.astype(jnp.float32) + part_b.astype(jnp.float32) + b_enc[:, None]
    feat = (jax.nn.softplus(4.0 * pre) / 4.0).astype(jnp.bfloat16)

    recon, (*acts_b, feat_b) = scattered(blocked_dot(dec_r, feat), [*jnp.split(acts_other, 4), feat])
    err = (recon + bias_both.astype(jnp.float32) - start.astype(jnp.float32)).astype(jnp.bfloat16)

    err_p = gathered(err)
    term = gathered_dot(dec_rt, err_p)
    term, err_p, err = lax.optimization_barrier((term, err_p, err))
    term_b = other_layer(term)
    err_own, err_other = placed(rows, err_p)
    term_b, err_own, err_other = lax.optimization_barrier((term_b, err_own, err_other))
    err_b = other_core(err_other)
    sums = jnp.sum(err.astype(jnp.float32), axis=1)
    width = sums.shape[0] // 2
    grad_bdec = scale * (sums[:width] + other_core(sums[width:]))
    grad_dec = outer_dec(feat, err_own, feat_b, err_b, scale)

    grad_feat = scale * (term.astype(jnp.float32) + term_b.astype(jnp.float32))
    grad_pre = grad_feat * jax.nn.sigmoid(4.0 * pre)
    grad_pre_b = grad_pre.astype(jnp.bfloat16)
    grad_pre_o = other_core(grad_pre_b)
    part_benc = jnp.sum(grad_pre, axis=1)
    grad_benc = part_benc + other_core(part_benc)
    grad_enc = outer_enc(acts_own, grad_pre_b, acts_b, grad_pre_o)
    return (grad_enc[None], grad_dec[None], grad_benc, grad_bdec[None])


def solution(mesh):
    finer = Mesh(mesh.devices.reshape(2, 2, 4, 4, 4), AXES)
    layer = ("z_lo", "core")
    return jax.shard_map(
        body,
        mesh=finer,
        in_specs=(
            P(layer, None, LATENT),
            P(layer, None, LATENT),
            P(LATENT),
            P(layer, LATENT, None),
            P(layer, LATENT),
        ),
        out_specs=(
            P(layer, None, LATENT),
            P(layer, LATENT, None),
            P(LATENT),
            P(layer, LATENT),
        ),
        check_vma=False,
    )
```

```python
import functools

import jax
import jax.numpy as jnp
import numpy as np
from jax import lax
from jax.experimental import pallas as pl
from jax.experimental.pallas import tpu as pltpu
from jax.sharding import Mesh
from jax.sharding import PartitionSpec as P

AXES = ("z_lo", "core", "x", "z_hi", "y")
LATENT = ("x", "z_hi", "y")
PLANE = ("core", "x", "y")
SPACE = ("core", "x", "z_hi", "y")
GROUPS = [
    [((c * 4 + (i if c == 0 else j)) * 4 + z) * 4 + (j if c == 0 else i) for i in range(4) for z in range(4)]
    for c in range(2)
    for j in range(4)
]
ORDER = (2, 1, 3)
BLOCK = 32

VMEM = pl.BlockSpec(memory_space=pltpu.VMEM)
SMEM = pl.BlockSpec(memory_space=pltpu.SMEM)
PARAMS = pltpu.CompilerParams(vmem_limit_bytes=16 * 1024 * 1024)


def other_core(x):
    return lax.ppermute(x, "core", [(0, 1), (1, 0)])


def other_layer(x):
    return lax.ppermute(x, "z_lo", [(0, 1), (1, 0)])


def among_sixteen(x):
    return lax.all_to_all(x, SPACE, 0, 0, axis_index_groups=GROUPS, tiled=True)


def along_last(x, k):
    pairs = []
    for c in range(2):
        for i in range(4):
            for j in range(4):
                a, b = (i, j ^ k) if c == 0 else (i ^ k, j)
                pairs.append((c * 16 + i * 4 + j, c * 16 + a * 4 + b))
    return lax.ppermute(x, PLANE, pairs)


def received(pieces):
    got = {k: along_last(pieces[k], k) for k in ORDER}
    return [pieces[0], got[1], got[2], got[3]]


def gathered(x):
    x = among_sixteen(jnp.broadcast_to(x[None], (16, *x.shape)))
    return received([x.reshape(-1, x.shape[-1])] * 4)


def summed(pieces):
    return sum(p.astype(jnp.float32) for p in pieces)


def scattered(pieces):
    total = summed(received(pieces)).astype(jnp.bfloat16)
    blocks = among_sixteen(total.reshape(16, -1, total.shape[-1]))
    return jnp.sum(blocks.astype(jnp.float32), axis=0)


def block_rows():
    c = lax.axis_index("core")
    x, y = lax.axis_index("x"), lax.axis_index("y")
    k = np.arange(64)
    last, near, up = k // 16, (k // 4) % 4, k % 4
    bx = jnp.where(c == 0, near, last ^ x)
    by = jnp.where(c == 0, last ^ y, near)
    return (BLOCK * (bx * 16 + up * 4 + by)).astype(jnp.int32)


def relative_enc_kernel(rows, own, other, out, blocks):
    step = pl.program_id(0)
    for k in range(16):
        at = pl.ds(pl.multiple_of(rows[step * 16 + k], BLOCK), BLOCK)
        blocks[2 * k * BLOCK : (2 * k + 1) * BLOCK, :] = own[at, :]
        blocks[(2 * k + 1) * BLOCK : (2 * k + 2) * BLOCK, :] = other[at, :]
    out[0] = blocks[...].T


def relative_enc(rows, own, other):
    depth, n = own.shape
    whole = pl.BlockSpec((depth, n), lambda i: (0, 0))
    return pl.pallas_call(
        relative_enc_kernel,
        out_shape=jax.ShapeDtypeStruct((4, n, depth // 2), jnp.bfloat16),
        grid=(4,),
        in_specs=[SMEM, whole, whole],
        out_specs=pl.BlockSpec((1, n, depth // 2), lambda i: (i, 0, 0)),
        scratch_shapes=[pltpu.VMEM((depth // 2, n), jnp.bfloat16)],
        compiler_params=PARAMS,
        cost_estimate=pl.CostEstimate(flops=1 << 20, bytes_accessed=16 << 20, transcendentals=0),
    )(rows, own, other)


def relative_dec_kernel(rows, own, other, out, own_t, other_t):
    @pl.when(pl.program_id(0) == 0)
    def _():
        width = own.shape[1]
        for j in range(0, width, 512):
            own_t[j : j + 512, :] = own[:, j : j + 512].T
            other_t[j : j + 512, :] = other[:, j : j + 512].T

    step = pl.program_id(0)
    for k in range(16):
        at = pl.ds(pl.multiple_of(rows[step * 16 + k], BLOCK), BLOCK)
        out[0, 2 * k * BLOCK : (2 * k + 1) * BLOCK, :] = own_t[at, :]
        out[0, (2 * k + 1) * BLOCK : (2 * k + 2) * BLOCK, :] = other_t[at, :]


def relative_dec(rows, own, other):
    n, width = own.shape
    whole = pl.BlockSpec((n, width), lambda i: (0, 0))
    return pl.pallas_call(
        relative_dec_kernel,
        out_shape=jax.ShapeDtypeStruct((4, width // 2, n), jnp.bfloat16),
        grid=(4,),
        in_specs=[SMEM, whole, whole],
        out_specs=pl.BlockSpec((1, width // 2, n), lambda i: (i, 0, 0)),
        scratch_shapes=[pltpu.VMEM((width, n), jnp.bfloat16)] * 2,
        compiler_params=PARAMS,
        cost_estimate=pl.CostEstimate(flops=1 << 20, bytes_accessed=16 << 20, transcendentals=0),
    )(rows, own, other)


def turned_kernel(x, out):
    out[0] = x[0].T


def turned(x):
    m, n = x.shape[1:]
    return pl.pallas_call(
        turned_kernel,
        out_shape=jax.ShapeDtypeStruct((4, n, m), jnp.bfloat16),
        grid=(4,),
        in_specs=[pl.BlockSpec((1, m, n), lambda i: (i, 0, 0))],
        out_specs=pl.BlockSpec((1, n, m), lambda i: (i, 0, 0)),
        compiler_params=PARAMS,
        cost_estimate=pl.CostEstimate(flops=1 << 20, bytes_accessed=16 << 20, transcendentals=0),
    )(x)


def gathered_dot_kernel(w, p0, p1, p2, p3, out):
    terms = [
        jnp.dot(w[k], p[...], preferred_element_type=jnp.float32)
        for k, p in enumerate((p0, p1, p2, p3))
    ]
    out[...] = (terms[0] + terms[1] + terms[2] + terms[3]).astype(out.dtype)


def gathered_dot(w, pieces):
    _, n, depth = w.shape
    tokens = pieces[0].shape[1]
    return pl.pallas_call(
        gathered_dot_kernel,
        out_shape=jax.ShapeDtypeStruct((n, tokens), jnp.bfloat16),
        in_specs=[VMEM] * 5,
        out_specs=VMEM,
        compiler_params=PARAMS,
        cost_estimate=pl.CostEstimate(
            flops=8 * n * depth * tokens, bytes_accessed=8 << 20, transcendentals=0
        ),
    )(w, *pieces)


def blocked_dot_kernel(w, feat, *pieces):
    for k, piece in enumerate(pieces):
        piece[...] = jnp.dot(w[k], feat[...], preferred_element_type=jnp.float32).astype(
            piece.dtype
        )


def blocked_dot(w, feat):
    _, width, n = w.shape
    tokens = feat.shape[1]
    piece = jax.ShapeDtypeStruct((width, tokens), jnp.bfloat16)
    return pl.pallas_call(
        blocked_dot_kernel,
        out_shape=(piece,) * 4,
        in_specs=[VMEM] * 2,
        out_specs=(VMEM,) * 4,
        compiler_params=PARAMS,
        cost_estimate=pl.CostEstimate(
            flops=8 * n * width * tokens, bytes_accessed=7 << 20, transcendentals=0
        ),
    )(w, feat)


def placed_kernel(rows, p0, p1, p2, p3, own, other):
    for k in range(64):
        at = pl.ds(pl.multiple_of(rows[k], BLOCK), BLOCK)
        piece, src = (p0, p1, p2, p3)[k // 16], (k % 16) * 2 * BLOCK
        own[at, :] = piece[src : src + BLOCK, :]
        other[at, :] = piece[src + BLOCK : src + 2 * BLOCK, :]


def placed(rows, pieces):
    depth, tokens = pieces[0].shape
    whole = jax.ShapeDtypeStruct((2 * depth, tokens), jnp.bfloat16)
    return pl.pallas_call(
        placed_kernel,
        out_shape=(whole, whole),
        in_specs=[SMEM] + [VMEM] * 4,
        out_specs=(VMEM,) * 2,
        compiler_params=PARAMS,
        cost_estimate=pl.CostEstimate(flops=1 << 20, bytes_accessed=4 << 20, transcendentals=0),
    )(rows, *pieces)


def dot_nt(a, b):
    return lax.dot_general(a, b, (((1,), (1,)), ((), ())), preferred_element_type=jnp.float32)


def outer_dec_kernel(scale, feat, err, feat_b, err_b, out):
    out[...] = (scale * (dot_nt(feat[...], err[...]) + dot_nt(feat_b[...], err_b[...]))).astype(
        out.dtype
    )


def outer_dec(feat, err, feat_b, err_b, scale):
    m, tokens = feat.shape
    n = err.shape[0]
    tile = n // 4
    left = pl.BlockSpec((m, tokens), lambda i: (0, 0))
    right = pl.BlockSpec((tile, tokens), lambda i: (i, 0))
    return pl.pallas_call(
        functools.partial(outer_dec_kernel, scale),
        out_shape=jax.ShapeDtypeStruct((m, n), jnp.bfloat16),
        grid=(4,),
        in_specs=[left, right, left, right],
        out_specs=pl.BlockSpec((m, tile), lambda i: (0, i)),
        compiler_params=PARAMS,
        cost_estimate=pl.CostEstimate(
            flops=40 * m * n * tokens, bytes_accessed=5 << 20, transcendentals=0
        ),
    )(feat, err, feat_b, err_b)


def outer_enc_kernel(acts, grad, acts_b, grad_b, out, sums):
    out[...] = (dot_nt(acts[...], grad[...]) + dot_nt(acts_b[...], grad_b[...])).astype(out.dtype)

    @pl.when(pl.program_id(0) == 0)
    def _():
        ones = jnp.ones((8, grad.shape[1]), grad.dtype)
        sums[...] = (dot_nt(ones, grad[...]) + dot_nt(ones, grad_b[...]))[:1]


def outer_enc(acts, grad, acts_b, grad_b):
    m, tokens = acts.shape
    n = grad.shape[0]
    tile = m // 4
    rows = pl.BlockSpec((tile, tokens), lambda i: (i, 0))
    whole = pl.BlockSpec((n, tokens), lambda i: (0, 0))
    return pl.pallas_call(
        outer_enc_kernel,
        out_shape=(
            jax.ShapeDtypeStruct((m, n), jnp.bfloat16),
            jax.ShapeDtypeStruct((1, n), jnp.float32),
        ),
        grid=(4,),
        in_specs=[rows, whole, rows, whole],
        out_specs=(
            pl.BlockSpec((tile, n), lambda i: (i, 0)),
            pl.BlockSpec((1, n), lambda i: (0, 0)),
        ),
        compiler_params=PARAMS,
        cost_estimate=pl.CostEstimate(
            flops=40 * m * n * tokens, bytes_accessed=5 << 20, transcendentals=0
        ),
    )(acts, grad, acts_b, grad_b)


def body(acts, w_enc, b_enc, w_dec, b_dec):
    tokens_all = acts.shape[1]
    half = tokens_all // 2
    scale = tokens_all ** (-0.5)
    core = lax.axis_index("core")
    rows = block_rows()

    local = acts[0].T
    swapped = other_core(local)
    start = jnp.concatenate(
        [lax.dynamic_slice_in_dim(a, core * half, half, 1) for a in (local, swapped)], axis=0
    )

    start, enc, dec, bias = lax.optimization_barrier((start, w_enc[0], w_dec[0], b_dec))
    enc_other, dec_other, bias_other = other_core(enc), other_core(dec), other_core(bias)
    enc_r = relative_enc(rows, enc, enc_other)
    dec_r = relative_dec(rows, dec, dec_other)
    acts_p = gathered(start)
    dec_rt = turned(dec_r)

    part = gathered_dot(enc_r, acts_p)
    part, acts_p = lax.optimization_barrier((part, acts_p))
    part_b = other_layer(part)
    acts_own, acts_other = placed(rows, acts_p)
    acts_b = other_core(acts_other)
    part_b, acts_b = lax.optimization_barrier((part_b, acts_b))
    pre = part.astype(jnp.float32) + part_b.astype(jnp.float32) + b_enc[:, None]
    feat = (jax.nn.softplus(4.0 * pre) / 4.0).astype(jnp.bfloat16)

    recon = scattered(blocked_dot(dec_r, feat))
    bias_both = jnp.concatenate([bias[0], bias_other[0]])[:, None]
    err = (recon + bias_both.astype(jnp.float32) - start.astype(jnp.float32)).astype(jnp.bfloat16)

    err_p = gathered(err)
    term = gathered_dot(dec_rt, err_p)
    term, err_p, feat, err = lax.optimization_barrier((term, err_p, feat, err))
    term_b = other_layer(term)
    err_own, err_other = placed(rows, err_p)
    err_b, feat_b = other_core(err_other), other_core(feat)
    sums = jnp.sum(err.astype(jnp.float32), axis=1)
    width = sums.shape[0] // 2
    grad_bdec = scale * (sums[:width] + other_core(sums[width:]))
    grad_dec = outer_dec(feat, err_own, feat_b, err_b, scale)
    term_b, grad_dec, grad_bdec = lax.optimization_barrier((term_b, grad_dec, grad_bdec))

    grad_feat = scale * (term.astype(jnp.float32) + term_b.astype(jnp.float32))
    grad_pre = (grad_feat * jax.nn.sigmoid(4.0 * pre)).astype(jnp.bfloat16)
    grad_enc, grad_benc = outer_enc(acts_own, grad_pre, acts_b, other_core(grad_pre))
    grad_benc = grad_benc[0]
    return (grad_enc[None], grad_dec[None], grad_benc, grad_bdec[None])


def solution(mesh):
    finer = Mesh(mesh.devices.reshape(2, 2, 4, 4, 4), AXES)
    layer = ("z_lo", "core")
    return jax.shard_map(
        body,
        mesh=finer,
        in_specs=(
            P(layer, None, LATENT),
            P(layer, None, LATENT),
            P(LATENT),
            P(layer, LATENT, None),
            P(layer, LATENT),
        ),
        out_specs=(
            P(layer, None, LATENT),
            P(layer, LATENT, None),
            P(LATENT),
            P(layer, LATENT),
        ),
        check_vma=False,
    )
```

```python
import functools

import jax
import jax.numpy as jnp
import numpy as np
from jax import lax
from jax.experimental import pallas as pl
from jax.experimental.pallas import tpu as pltpu
from jax.sharding import Mesh
from jax.sharding import PartitionSpec as P

AXES = ("z_lo", "core", "x", "z_hi", "y")
LATENT = ("x", "z_hi", "y")
PLANE = ("core", "x", "y")
SPACE = ("core", "x", "z_hi", "y")
GROUPS = [
    [((c * 4 + (i if c == 0 else j)) * 4 + z) * 4 + (j if c == 0 else i) for i in range(4) for z in range(4)]
    for c in range(2)
    for j in range(4)
]
ORDER = (2, 1, 3)
BLOCK = 32

VMEM = pl.BlockSpec(memory_space=pltpu.VMEM)
SMEM = pl.BlockSpec(memory_space=pltpu.SMEM)
PARAMS = pltpu.CompilerParams(vmem_limit_bytes=16 * 1024 * 1024)
SMALL = pltpu.CompilerParams(vmem_limit_bytes=6 * 1024 * 1024)


def other_core(x):
    return lax.ppermute(x, "core", [(0, 1), (1, 0)])


def other_layer(x):
    return lax.ppermute(x, "z_lo", [(0, 1), (1, 0)])


def among_sixteen(x):
    return lax.all_to_all(x, SPACE, 0, 0, axis_index_groups=GROUPS, tiled=True)


def in_plane(x, k, x_core):
    pairs = []
    for c in range(2):
        for i in range(4):
            for j in range(4):
                a, b = (i ^ k, j) if c == x_core else (i, j ^ k)
                pairs.append((c * 16 + i * 4 + j, c * 16 + a * 4 + b))
    return lax.ppermute(x, PLANE, pairs)


def along_last(x, k):
    return in_plane(x, k, 1)


def received(pieces):
    got = {k: along_last(pieces[k], k) for k in ORDER}
    return [pieces[0], got[1], got[2], got[3]]


def along_z(x, k):
    return lax.ppermute(x, "z_hi", [(i, i ^ k) for i in range(4)])


def along_first(x, k):
    return in_plane(x, k, 0)


def in_two(x):
    return [received([g] * 4) for g in jnp.split(x, 2, axis=1)]


def gathered(x):
    x = among_sixteen(jnp.broadcast_to(x[None], (16, *x.shape)))
    return in_two(x.reshape(-1, x.shape[-1]))


def gathered_by_permutes(x):
    for send in (along_z, along_first):
        got = {k: send(x, k) for k in ORDER}
        x = jnp.concatenate([x, got[1], got[2], got[3]], axis=0)
    return in_two(x)


def summed(pieces):
    return sum(p.astype(jnp.float32) for p in pieces)


def scattered(parts):
    total = [summed(received(pieces)).astype(jnp.bfloat16) for pieces in parts]
    total = jnp.concatenate(total, axis=1)
    blocks = among_sixteen(total.reshape(16, -1, total.shape[-1]))
    return jnp.sum(blocks.astype(jnp.float32), axis=0)


def block_rows(relative):
    c = lax.axis_index("core")
    x, z, y = (lax.axis_index(a) for a in LATENT)
    k = np.arange(64)
    last, near, up = k // 16, (k // 4) % 4, k % 4
    if relative:
        bx = jnp.where(c == 0, near ^ x, last ^ x)
        by = jnp.where(c == 0, last ^ y, near ^ y)
        bz = up ^ z
    else:
        bx = jnp.where(c == 0, near, last ^ x)
        by = jnp.where(c == 0, last ^ y, near)
        bz = up
    return (BLOCK * (bx * 16 + bz * 4 + by)).astype(jnp.int32)


def relative_enc_kernel(rows, own, other, out, blocks):
    step = pl.program_id(0)
    for k in range(16):
        at = pl.ds(pl.multiple_of(rows[step * 16 + k], BLOCK), BLOCK)
        blocks[2 * k * BLOCK : (2 * k + 1) * BLOCK, :] = own[at, :]
        blocks[(2 * k + 1) * BLOCK : (2 * k + 2) * BLOCK, :] = other[at, :]
    out[0] = blocks[...].T


def relative_enc(rows, own, other):
    depth, n = own.shape
    whole = pl.BlockSpec((depth, n), lambda i: (0, 0))
    return pl.pallas_call(
        relative_enc_kernel,
        out_shape=jax.ShapeDtypeStruct((4, n, depth // 2), jnp.bfloat16),
        grid=(4,),
        in_specs=[SMEM, whole, whole],
        out_specs=pl.BlockSpec((1, n, depth // 2), lambda i: (i, 0, 0)),
        scratch_shapes=[pltpu.VMEM((depth // 2, n), jnp.bfloat16)],
        compiler_params=PARAMS,
        cost_estimate=pl.CostEstimate(flops=1 << 20, bytes_accessed=16 << 20, transcendentals=0),
    )(rows, own, other)


def relative_dec_kernel(rows, own, other, out, own_t, other_t):
    @pl.when(pl.program_id(0) == 0)
    def _():
        width = own.shape[1]
        for j in range(0, width, 512):
            own_t[j : j + 512, :] = own[:, j : j + 512].T
            other_t[j : j + 512, :] = other[:, j : j + 512].T

    step = pl.program_id(0)
    for k in range(16):
        at = pl.ds(pl.multiple_of(rows[step * 16 + k], BLOCK), BLOCK)
        out[0, 2 * k * BLOCK : (2 * k + 1) * BLOCK, :] = own_t[at, :]
        out[0, (2 * k + 1) * BLOCK : (2 * k + 2) * BLOCK, :] = other_t[at, :]


def relative_dec(rows, own, other):
    n, width = own.shape
    whole = pl.BlockSpec((n, width), lambda i: (0, 0))
    return pl.pallas_call(
        relative_dec_kernel,
        out_shape=jax.ShapeDtypeStruct((4, width // 2, n), jnp.bfloat16),
        grid=(4,),
        in_specs=[SMEM, whole, whole],
        out_specs=pl.BlockSpec((1, width // 2, n), lambda i: (i, 0, 0)),
        scratch_shapes=[pltpu.VMEM((width, n), jnp.bfloat16)] * 2,
        compiler_params=PARAMS,
        cost_estimate=pl.CostEstimate(flops=1 << 20, bytes_accessed=16 << 20, transcendentals=0),
    )(rows, own, other)


def turned_kernel(x, out):
    out[0] = x[0].T


def turned(x):
    m, n = x.shape[1:]
    return pl.pallas_call(
        turned_kernel,
        out_shape=jax.ShapeDtypeStruct((4, n, m), jnp.bfloat16),
        grid=(4,),
        in_specs=[pl.BlockSpec((1, m, n), lambda i: (i, 0, 0))],
        out_specs=pl.BlockSpec((1, n, m), lambda i: (i, 0, 0)),
        compiler_params=PARAMS,
        cost_estimate=pl.CostEstimate(flops=1 << 20, bytes_accessed=16 << 20, transcendentals=0),
    )(x)


def gathered_dot_kernel(w, p0, p1, p2, p3, out):
    terms = [
        jnp.dot(w[k], p[...], preferred_element_type=jnp.float32)
        for k, p in enumerate((p0, p1, p2, p3))
    ]
    out[...] = (terms[0] + terms[1] + terms[2] + terms[3]).astype(out.dtype)


def gathered_dot(w, pieces):
    _, n, depth = w.shape
    tokens = pieces[0].shape[1]
    return pl.pallas_call(
        gathered_dot_kernel,
        out_shape=jax.ShapeDtypeStruct((n, tokens), jnp.bfloat16),
        in_specs=[VMEM] * 5,
        out_specs=VMEM,
        compiler_params=SMALL,
        cost_estimate=pl.CostEstimate(
            flops=8 * n * depth * tokens, bytes_accessed=8 << 20, transcendentals=0
        ),
    )(w, *pieces)


def blocked_dot_kernel(w, part, part_b, bias, feat, *pieces):
    pre = part[...].astype(jnp.float32) + part_b[...].astype(jnp.float32) + bias[...]
    feat[...] = (jax.nn.softplus(4.0 * pre) / 4.0).astype(feat.dtype)
    for k in ORDER + (0,):
        pieces[k][...] = jnp.dot(w[k], feat[...], preferred_element_type=jnp.float32).astype(
            feat.dtype
        )


def blocked_dot(w, part, part_b, bias):
    _, width, n = w.shape
    tokens = part.shape[1]
    piece = jax.ShapeDtypeStruct((width, tokens), jnp.bfloat16)
    feat, *pieces = pl.pallas_call(
        blocked_dot_kernel,
        out_shape=(jax.ShapeDtypeStruct((n, tokens), jnp.bfloat16),) + (piece,) * 4,
        in_specs=[VMEM] * 4,
        out_specs=(VMEM,) * 5,
        compiler_params=SMALL,
        cost_estimate=pl.CostEstimate(
            flops=1 << 20, bytes_accessed=1 << 20, transcendentals=0
        ),
    )(w, part, part_b, bias)
    return feat, pieces


def placed_kernel(rows, *refs):
    pieces, (own, other) = refs[:-2], refs[-2:]
    tokens = pieces[0].shape[1]
    for k in range(64):
        at = pl.ds(pl.multiple_of(rows[k], BLOCK), BLOCK)
        src = (k % 16) * 2 * BLOCK
        for half in range(2):
            piece, to = pieces[half * 4 + k // 16], slice(half * tokens, (half + 1) * tokens)
            own[at, to] = piece[src : src + BLOCK, :]
            other[at, to] = piece[src + BLOCK : src + 2 * BLOCK, :]


def placed(rows, parts):
    depth, tokens = parts[0][0].shape
    whole = jax.ShapeDtypeStruct((2 * depth, 2 * tokens), jnp.bfloat16)
    return pl.pallas_call(
        placed_kernel,
        out_shape=(whole, whole),
        in_specs=[SMEM] + [VMEM] * 8,
        out_specs=(VMEM,) * 2,
        compiler_params=SMALL,
        cost_estimate=pl.CostEstimate(flops=1 << 20, bytes_accessed=4 << 20, transcendentals=0),
    )(rows, *parts[0], *parts[1])


def dot_nt(a, b):
    return lax.dot_general(a, b, (((1,), (1,)), ((), ())), preferred_element_type=jnp.float32)


def outer_dec_kernel(scale, feat, err, feat_b, err_b, out):
    out[...] = (scale * (dot_nt(feat[...], err[...]) + dot_nt(feat_b[...], err_b[...]))).astype(
        out.dtype
    )


def outer_dec(feat, err, feat_b, err_b, scale):
    m, tokens = feat.shape
    n = err.shape[0]
    tile = n // 4
    left = pl.BlockSpec((m, tokens), lambda i: (0, 0))
    right = pl.BlockSpec((tile, tokens), lambda i: (i, 0))
    return pl.pallas_call(
        functools.partial(outer_dec_kernel, scale),
        out_shape=jax.ShapeDtypeStruct((m, n), jnp.bfloat16),
        grid=(4,),
        in_specs=[left, right, left, right],
        out_specs=pl.BlockSpec((m, tile), lambda i: (0, i)),
        compiler_params=PARAMS,
        cost_estimate=pl.CostEstimate(
            flops=4 * m * n * tokens, bytes_accessed=5 << 20, transcendentals=0
        ),
    )(feat, err, feat_b, err_b)


def outer_enc_kernel(acts, grad, acts_b, grad_b, out, sums):
    out[...] = (dot_nt(acts[...], grad[...]) + dot_nt(acts_b[...], grad_b[...])).astype(out.dtype)

    @pl.when(pl.program_id(0) == 0)
    def _():
        ones = jnp.ones((8, grad.shape[1]), grad.dtype)
        sums[...] = (dot_nt(ones, grad[...]) + dot_nt(ones, grad_b[...]))[:1]


def outer_enc(acts, grad, acts_b, grad_b):
    m, tokens = acts.shape
    n = grad.shape[0]
    tile = m // 4
    rows = pl.BlockSpec((tile, tokens), lambda i: (i, 0))
    whole = pl.BlockSpec((n, tokens), lambda i: (0, 0))
    return pl.pallas_call(
        outer_enc_kernel,
        out_shape=(
            jax.ShapeDtypeStruct((m, n), jnp.bfloat16),
            jax.ShapeDtypeStruct((1, n), jnp.float32),
        ),
        grid=(4,),
        in_specs=[rows, whole, rows, whole],
        out_specs=(
            pl.BlockSpec((tile, n), lambda i: (i, 0)),
            pl.BlockSpec((1, n), lambda i: (0, 0)),
        ),
        compiler_params=PARAMS,
        cost_estimate=pl.CostEstimate(
            flops=40 * m * n * tokens, bytes_accessed=5 << 20, transcendentals=0
        ),
    )(acts, grad, acts_b, grad_b)


def body(acts, w_enc, b_enc, w_dec, b_dec):
    tokens_all = acts.shape[1]
    half = tokens_all // 2
    scale = tokens_all ** (-0.5)
    core = lax.axis_index("core")
    rows, acts_rows = block_rows(False), block_rows(True)

    local = acts[0].T
    swapped = other_core(local)
    start = jnp.concatenate(
        [lax.dynamic_slice_in_dim(a, core * half, half, 1) for a in (local, swapped)], axis=0
    )

    start, enc, dec, bias = lax.optimization_barrier((start, w_enc[0], w_dec[0], b_dec))
    enc_other, dec_other, bias_other = other_core(enc), other_core(dec), other_core(bias)
    enc_r = relative_enc(acts_rows, enc, enc_other)
    dec_r = relative_dec(rows, dec, dec_other)
    acts_p = gathered_by_permutes(start)
    dec_rt = turned(dec_r)

    enc_r, dec_r = lax.optimization_barrier((enc_r, dec_r))
    part = [gathered_dot(enc_r, pieces) for pieces in acts_p]
    part_b = [other_layer(part[0]), None]
    part_b[0], part[1], acts_p = lax.optimization_barrier((part_b[0], part[1], acts_p))
    part_b[1] = other_layer(part[1])
    acts_own, acts_other = placed(acts_rows, acts_p)
    acts_b = other_core(acts_other)
    part_b[1], acts_b = lax.optimization_barrier((part_b[1], acts_b))
    b_lanes = jnp.broadcast_to(b_enc[:, None], part[0].shape)
    feats, recon = zip(*(blocked_dot(dec_r, p, q, b_lanes) for p, q in zip(part, part_b)))
    recon = scattered(recon)
    feat = jnp.concatenate(feats, axis=1)
    bias_both = jnp.concatenate([bias[0], bias_other[0]])[:, None]
    err = (recon + bias_both.astype(jnp.float32) - start.astype(jnp.float32)).astype(jnp.bfloat16)

    err_p = gathered(err)
    term = [gathered_dot(dec_rt, pieces) for pieces in err_p]
    term_b = [other_layer(term[0]), None]
    term_b[0], term[1], err_p, feat, err = lax.optimization_barrier(
        (term_b[0], term[1], err_p, feat, err)
    )
    term_b[1] = other_layer(term[1])
    err_own, err_other = placed(rows, err_p)
    err_b, feat_b = other_core(err_other), other_core(feat)
    sums = jnp.sum(err.astype(jnp.float32), axis=1)
    width = sums.shape[0] // 2
    grad_bdec = scale * (sums[:width] + other_core(sums[width:]))
    grad_dec = outer_dec(feat, err_own, feat_b, err_b, scale)
    term_b[1], grad_dec, grad_bdec = lax.optimization_barrier((term_b[1], grad_dec, grad_bdec))

    pre = [
        p.astype(jnp.float32) + q.astype(jnp.float32) + b_enc[:, None] for p, q in zip(part, part_b)
    ]
    grad_pre = [
        (scale * (t.astype(jnp.float32) + u.astype(jnp.float32)) * jax.nn.sigmoid(4.0 * p)).astype(
            jnp.bfloat16
        )
        for t, u, p in zip(term, term_b, pre)
    ]
    grad_pre = jnp.concatenate(grad_pre, axis=1)
    grad_enc, grad_benc = outer_enc(acts_own, grad_pre, acts_b, other_core(grad_pre))
    grad_benc = grad_benc[0]
    return (grad_enc[None], grad_dec[None], grad_benc, grad_bdec[None])


def solution(mesh):
    finer = Mesh(mesh.devices.reshape(2, 2, 4, 4, 4), AXES)
    layer = ("z_lo", "core")
    return jax.shard_map(
        body,
        mesh=finer,
        in_specs=(
            P(layer, None, LATENT),
            P(layer, None, LATENT),
            P(LATENT),
            P(layer, LATENT, None),
            P(layer, LATENT),
        ),
        out_specs=(
            P(layer, None, LATENT),
            P(layer, LATENT, None),
            P(LATENT),
            P(layer, LATENT),
        ),
        check_vma=False,
    )
```

```python
import functools

import jax
import jax.numpy as jnp
import numpy as np
from jax import lax
from jax.experimental import pallas as pl
from jax.experimental.pallas import tpu as pltpu
from jax.sharding import Mesh
from jax.sharding import PartitionSpec as P

AXES = ("z_lo", "core", "x", "z_hi", "y")
LATENT = ("x", "z_hi", "y")
PLANE = ("core", "x", "y")
SPACE = ("core", "x", "z_hi", "y")
GROUPS = [
    [((c * 4 + (i if c == 0 else j)) * 4 + z) * 4 + (j if c == 0 else i) for i in range(4) for z in range(4)]
    for c in range(2)
    for j in range(4)
]
ORDER = (2, 1, 3)
BLOCK = 32

VMEM = pl.BlockSpec(memory_space=pltpu.VMEM)
SMEM = pl.BlockSpec(memory_space=pltpu.SMEM)
PARAMS = pltpu.CompilerParams(vmem_limit_bytes=16 * 1024 * 1024)
SMALL = pltpu.CompilerParams(vmem_limit_bytes=6 * 1024 * 1024)


def other_core(x):
    return lax.ppermute(x, "core", [(0, 1), (1, 0)])


def other_layer(x):
    return lax.ppermute(x, "z_lo", [(0, 1), (1, 0)])


def among_sixteen(x):
    return lax.all_to_all(x, SPACE, 0, 0, axis_index_groups=GROUPS, tiled=True)


def in_plane(x, k, x_core):
    pairs = []
    for c in range(2):
        for i in range(4):
            for j in range(4):
                a, b = (i ^ k, j) if c == x_core else (i, j ^ k)
                pairs.append((c * 16 + i * 4 + j, c * 16 + a * 4 + b))
    return lax.ppermute(x, PLANE, pairs)


def along_last(x, k):
    return in_plane(x, k, 1)


def received(pieces):
    got = {k: along_last(pieces[k], k) for k in ORDER}
    return [pieces[0], got[1], got[2], got[3]]


def along_z(x, k):
    return lax.ppermute(x, "z_hi", [(i, i ^ k) for i in range(4)])


def along_first(x, k):
    return in_plane(x, k, 0)


def in_two(x):
    return [received([g] * 4) for g in jnp.split(x, 2, axis=1)]


def gathered(x):
    x = among_sixteen(jnp.broadcast_to(x[None], (16, *x.shape)))
    return in_two(x.reshape(-1, x.shape[-1]))


def gathered_by_permutes(x):
    for send in (along_z, along_first):
        got = {k: send(x, k) for k in ORDER}
        x = jnp.concatenate([x, got[1], got[2], got[3]], axis=0)
    return received([x] * 4)


def summed(pieces):
    return sum(p.astype(jnp.float32) for p in pieces)


def scattered(pieces):
    total = summed(received(pieces)).astype(jnp.bfloat16)
    blocks = among_sixteen(total.reshape(16, -1, total.shape[-1]))
    return jnp.sum(blocks.astype(jnp.float32), axis=0)


def block_rows(relative):
    c = lax.axis_index("core")
    x, z, y = (lax.axis_index(a) for a in LATENT)
    k = np.arange(64)
    last, near, up = k // 16, (k // 4) % 4, k % 4
    if relative:
        bx = jnp.where(c == 0, near ^ x, last ^ x)
        by = jnp.where(c == 0, last ^ y, near ^ y)
        bz = up ^ z
    else:
        bx = jnp.where(c == 0, near, last ^ x)
        by = jnp.where(c == 0, last ^ y, near)
        bz = up
    return (BLOCK * (bx * 16 + bz * 4 + by)).astype(jnp.int32)


def relative_enc_kernel(rows, own, other, out, blocks):
    step = pl.program_id(0)
    for k in range(16):
        at = pl.ds(pl.multiple_of(rows[step * 16 + k], BLOCK), BLOCK)
        blocks[2 * k * BLOCK : (2 * k + 1) * BLOCK, :] = own[at, :]
        blocks[(2 * k + 1) * BLOCK : (2 * k + 2) * BLOCK, :] = other[at, :]
    out[0] = blocks[...].T


def relative_enc(rows, own, other):
    depth, n = own.shape
    whole = pl.BlockSpec((depth, n), lambda i: (0, 0))
    return pl.pallas_call(
        relative_enc_kernel,
        out_shape=jax.ShapeDtypeStruct((4, n, depth // 2), jnp.bfloat16),
        grid=(4,),
        in_specs=[SMEM, whole, whole],
        out_specs=pl.BlockSpec((1, n, depth // 2), lambda i: (i, 0, 0)),
        scratch_shapes=[pltpu.VMEM((depth // 2, n), jnp.bfloat16)],
        compiler_params=PARAMS,
        cost_estimate=pl.CostEstimate(flops=1 << 20, bytes_accessed=16 << 20, transcendentals=0),
    )(rows, own, other)


def relative_dec_kernel(rows, own, other, out, own_t, other_t):
    @pl.when(pl.program_id(0) == 0)
    def _():
        width = own.shape[1]
        for j in range(0, width, 512):
            own_t[j : j + 512, :] = own[:, j : j + 512].T
            other_t[j : j + 512, :] = other[:, j : j + 512].T

    step = pl.program_id(0)
    for k in range(16):
        at = pl.ds(pl.multiple_of(rows[step * 16 + k], BLOCK), BLOCK)
        out[0, 2 * k * BLOCK : (2 * k + 1) * BLOCK, :] = own_t[at, :]
        out[0, (2 * k + 1) * BLOCK : (2 * k + 2) * BLOCK, :] = other_t[at, :]


def relative_dec(rows, own, other):
    n, width = own.shape
    whole = pl.BlockSpec((n, width), lambda i: (0, 0))
    return pl.pallas_call(
        relative_dec_kernel,
        out_shape=jax.ShapeDtypeStruct((4, width // 2, n), jnp.bfloat16),
        grid=(4,),
        in_specs=[SMEM, whole, whole],
        out_specs=pl.BlockSpec((1, width // 2, n), lambda i: (i, 0, 0)),
        scratch_shapes=[pltpu.VMEM((width, n), jnp.bfloat16)] * 2,
        compiler_params=PARAMS,
        cost_estimate=pl.CostEstimate(flops=1 << 20, bytes_accessed=16 << 20, transcendentals=0),
    )(rows, own, other)


def turned_kernel(x, out):
    out[0] = x[0].T


def turned(x):
    m, n = x.shape[1:]
    return pl.pallas_call(
        turned_kernel,
        out_shape=jax.ShapeDtypeStruct((4, n, m), jnp.bfloat16),
        grid=(4,),
        in_specs=[pl.BlockSpec((1, m, n), lambda i: (i, 0, 0))],
        out_specs=pl.BlockSpec((1, n, m), lambda i: (i, 0, 0)),
        compiler_params=PARAMS,
        cost_estimate=pl.CostEstimate(flops=1 << 20, bytes_accessed=16 << 20, transcendentals=0),
    )(x)


def gathered_dot_kernel(w, p0, p1, p2, p3, out):
    terms = [
        jnp.dot(w[k], p[...], preferred_element_type=jnp.float32)
        for k, p in enumerate((p0, p1, p2, p3))
    ]
    out[...] = (terms[0] + terms[1] + terms[2] + terms[3]).astype(out.dtype)


def gathered_dot(w, pieces):
    _, n, depth = w.shape
    tokens = pieces[0].shape[1]
    return pl.pallas_call(
        gathered_dot_kernel,
        out_shape=jax.ShapeDtypeStruct((n, tokens), jnp.bfloat16),
        in_specs=[VMEM] * 5,
        out_specs=VMEM,
        compiler_params=SMALL,
        cost_estimate=pl.CostEstimate(
            flops=8 * n * depth * tokens, bytes_accessed=8 << 20, transcendentals=0
        ),
    )(w, *pieces)


def blocked_dot_kernel(w, part, part_b, bias, feat, *pieces):
    pre = part[...].astype(jnp.float32) + part_b[...].astype(jnp.float32) + bias[...]
    feat[...] = (jax.nn.softplus(4.0 * pre) / 4.0).astype(feat.dtype)
    for k in ORDER + (0,):
        pieces[k][...] = jnp.dot(w[k], feat[...], preferred_element_type=jnp.float32).astype(
            feat.dtype
        )


def blocked_dot(w, part, part_b, bias):
    _, width, n = w.shape
    tokens = part.shape[1]
    piece = jax.ShapeDtypeStruct((width, tokens), jnp.bfloat16)
    feat, *pieces = pl.pallas_call(
        blocked_dot_kernel,
        out_shape=(jax.ShapeDtypeStruct((n, tokens), jnp.bfloat16),) + (piece,) * 4,
        in_specs=[VMEM] * 4,
        out_specs=(VMEM,) * 5,
        compiler_params=SMALL,
        cost_estimate=pl.CostEstimate(
            flops=1 << 20, bytes_accessed=1 << 20, transcendentals=0
        ),
    )(w, part, part_b, bias)
    return feat, pieces


def placed_kernel(rows, *refs):
    pieces, (own, other) = refs[:-2], refs[-2:]
    tokens = pieces[0].shape[1]
    for k in range(64):
        at = pl.ds(pl.multiple_of(rows[k], BLOCK), BLOCK)
        src = (k % 16) * 2 * BLOCK
        for part in range(len(pieces) // 4):
            piece, to = pieces[part * 4 + k // 16], slice(part * tokens, (part + 1) * tokens)
            own[at, to] = piece[src : src + BLOCK, :]
            other[at, to] = piece[src + BLOCK : src + 2 * BLOCK, :]


def placed(rows, parts):
    depth, tokens = parts[0][0].shape
    whole = jax.ShapeDtypeStruct((2 * depth, len(parts) * tokens), jnp.bfloat16)
    return pl.pallas_call(
        placed_kernel,
        out_shape=(whole, whole),
        in_specs=[SMEM] + [VMEM] * (4 * len(parts)),
        out_specs=(VMEM,) * 2,
        compiler_params=SMALL,
        cost_estimate=pl.CostEstimate(flops=1 << 20, bytes_accessed=4 << 20, transcendentals=0),
    )(rows, *(p for part in parts for p in part))


def dot_nt(a, b):
    return lax.dot_general(a, b, (((1,), (1,)), ((), ())), preferred_element_type=jnp.float32)


def outer_dec_kernel(scale, feat, err, feat_b, err_b, out):
    out[...] = (scale * (dot_nt(feat[...], err[...]) + dot_nt(feat_b[...], err_b[...]))).astype(
        out.dtype
    )


def outer_dec(feat, err, feat_b, err_b, scale):
    m, tokens = feat.shape
    n = err.shape[0]
    tile = n // 4
    left = pl.BlockSpec((m, tokens), lambda i: (0, 0))
    right = pl.BlockSpec((tile, tokens), lambda i: (i, 0))
    return pl.pallas_call(
        functools.partial(outer_dec_kernel, scale),
        out_shape=jax.ShapeDtypeStruct((m, n), jnp.bfloat16),
        grid=(4,),
        in_specs=[left, right, left, right],
        out_specs=pl.BlockSpec((m, tile), lambda i: (0, i)),
        compiler_params=PARAMS,
        cost_estimate=pl.CostEstimate(
            flops=4 * m * n * tokens, bytes_accessed=5 << 20, transcendentals=0
        ),
    )(feat, err, feat_b, err_b)


def outer_enc_kernel(acts, grad, acts_b, grad_b, out, sums):
    out[...] = (dot_nt(acts[...], grad[...]) + dot_nt(acts_b[...], grad_b[...])).astype(out.dtype)

    @pl.when(pl.program_id(0) == 0)
    def _():
        ones = jnp.ones((8, grad.shape[1]), grad.dtype)
        sums[...] = (dot_nt(ones, grad[...]) + dot_nt(ones, grad_b[...]))[:1]


def outer_enc(acts, grad, acts_b, grad_b):
    m, tokens = acts.shape
    n = grad.shape[0]
    tile = m // 4
    rows = pl.BlockSpec((tile, tokens), lambda i: (i, 0))
    whole = pl.BlockSpec((n, tokens), lambda i: (0, 0))
    return pl.pallas_call(
        outer_enc_kernel,
        out_shape=(
            jax.ShapeDtypeStruct((m, n), jnp.bfloat16),
            jax.ShapeDtypeStruct((1, n), jnp.float32),
        ),
        grid=(4,),
        in_specs=[rows, whole, rows, whole],
        out_specs=(
            pl.BlockSpec((tile, n), lambda i: (i, 0)),
            pl.BlockSpec((1, n), lambda i: (0, 0)),
        ),
        compiler_params=PARAMS,
        cost_estimate=pl.CostEstimate(
            flops=40 * m * n * tokens, bytes_accessed=5 << 20, transcendentals=0
        ),
    )(acts, grad, acts_b, grad_b)


def body(acts, w_enc, b_enc, w_dec, b_dec):
    tokens_all = acts.shape[1]
    half = tokens_all // 2
    scale = tokens_all ** (-0.5)
    core = lax.axis_index("core")
    rows, acts_rows = block_rows(False), block_rows(True)

    local = acts[0].T
    swapped = other_core(local)
    start = jnp.concatenate(
        [lax.dynamic_slice_in_dim(a, core * half, half, 1) for a in (local, swapped)], axis=0
    )

    start, enc, dec, bias = lax.optimization_barrier((start, w_enc[0], w_dec[0], b_dec))
    enc_other, dec_other, bias_other = other_core(enc), other_core(dec), other_core(bias)
    enc_r = relative_enc(acts_rows, enc, enc_other)
    dec_r = relative_dec(rows, dec, dec_other)
    acts_p = gathered_by_permutes(start)

    part = gathered_dot(enc_r, acts_p)
    part, acts_p = lax.optimization_barrier((part, acts_p))
    part_b = other_layer(part)
    acts_own, acts_other = placed(acts_rows, [acts_p])
    acts_b = other_core(acts_other)
    part_b, acts_b = lax.optimization_barrier((part_b, acts_b))
    b_lanes = jnp.broadcast_to(b_enc[:, None], part.shape)
    feat, recon = blocked_dot(dec_r, part, part_b, b_lanes)
    recon = scattered(recon)
    bias_both = jnp.concatenate([bias[0], bias_other[0]])[:, None]
    err = (recon + bias_both.astype(jnp.float32) - start.astype(jnp.float32)).astype(jnp.bfloat16)

    sums = jnp.sum(err.astype(jnp.float32), axis=1)
    width = sums.shape[0] // 2
    grad_bdec = scale * (sums[:width] + other_core(sums[width:]))
    err_p = gathered(err)
    err_p[0][2], dec_r = lax.optimization_barrier((err_p[0][2], dec_r))
    dec_rt = turned(dec_r)
    err_p[1], grad_bdec = lax.optimization_barrier((err_p[1], grad_bdec))
    term = [gathered_dot(dec_rt, pieces) for pieces in err_p]
    term_b = [other_layer(term[0]), None]
    term_b[0], term[1], err_p, feat = lax.optimization_barrier((term_b[0], term[1], err_p, feat))
    term_b[1] = other_layer(term[1])
    err_own, err_other = placed(rows, err_p)
    err_b, feat_b = other_core(err_other), other_core(feat)
    grad_dec = outer_dec(feat, err_own, feat_b, err_b, scale)
    term_b[1], grad_dec = lax.optimization_barrier((term_b[1], grad_dec))

    term, term_b = (jnp.concatenate(t, axis=1).astype(jnp.float32) for t in (term, term_b))
    pre = part.astype(jnp.float32) + part_b.astype(jnp.float32) + b_enc[:, None]
    grad_pre = (scale * (term + term_b) * jax.nn.sigmoid(4.0 * pre)).astype(jnp.bfloat16)
    grad_enc, grad_benc = outer_enc(acts_own, grad_pre, acts_b, other_core(grad_pre))
    grad_benc = grad_benc[0]
    return (grad_enc[None], grad_dec[None], grad_benc, grad_bdec[None])


def solution(mesh):
    finer = Mesh(mesh.devices.reshape(2, 2, 4, 4, 4), AXES)
    layer = ("z_lo", "core")
    return jax.shard_map(
        body,
        mesh=finer,
        in_specs=(
            P(layer, None, LATENT),
            P(layer, None, LATENT),
            P(LATENT),
            P(layer, LATENT, None),
            P(layer, LATENT),
        ),
        out_specs=(
            P(layer, None, LATENT),
            P(layer, LATENT, None),
            P(LATENT),
            P(layer, LATENT),
        ),
        check_vma=False,
    )
```

```python
import functools

import jax
import jax.numpy as jnp
import numpy as np
from jax import lax
from jax.experimental import pallas as pl
from jax.experimental.pallas import tpu as pltpu
from jax.sharding import Mesh
from jax.sharding import PartitionSpec as P

AXES = ("z_lo", "core", "x", "z_hi", "y")
LATENT = ("x", "z_hi", "y")
PLANE = ("core", "x", "y")
SPACE = ("core", "x", "z_hi", "y")
GROUPS = [
    [((c * 4 + (i if c == 0 else j)) * 4 + z) * 4 + (j if c == 0 else i) for i in range(4) for z in range(4)]
    for c in range(2)
    for j in range(4)
]
ORDER = (2, 1, 3)
BLOCK = 32

VMEM = pl.BlockSpec(memory_space=pltpu.VMEM)
SMEM = pl.BlockSpec(memory_space=pltpu.SMEM)
PARAMS = pltpu.CompilerParams(vmem_limit_bytes=16 * 1024 * 1024)
SMALL = pltpu.CompilerParams(vmem_limit_bytes=6 * 1024 * 1024)


def other_core(x):
    return lax.ppermute(x, "core", [(0, 1), (1, 0)])


def other_layer(x):
    return lax.ppermute(x, "z_lo", [(0, 1), (1, 0)])


def among_sixteen(x):
    return lax.all_to_all(x, SPACE, 0, 0, axis_index_groups=GROUPS, tiled=True)


def in_plane(x, k, x_core):
    pairs = []
    for c in range(2):
        for i in range(4):
            for j in range(4):
                a, b = (i ^ k, j) if c == x_core else (i, j ^ k)
                pairs.append((c * 16 + i * 4 + j, c * 16 + a * 4 + b))
    return lax.ppermute(x, PLANE, pairs)


def along_last(x, k):
    return in_plane(x, k, 1)


def received(pieces):
    got = {k: along_last(pieces[k], k) for k in ORDER}
    return [pieces[0], got[1], got[2], got[3]]


def along_z(x, k):
    return lax.ppermute(x, "z_hi", [(i, i ^ k) for i in range(4)])


def along_first(x, k):
    return in_plane(x, k, 0)


def in_two(x):
    return [received([g] * 4) for g in jnp.split(x, 2, axis=1)]


def gathered(x):
    x = among_sixteen(jnp.broadcast_to(x[None], (16, *x.shape)))
    return in_two(x.reshape(-1, x.shape[-1]))


def gathered_by_permutes(x):
    for send in (along_z, along_first):
        got = {k: send(x, k) for k in ORDER}
        x = jnp.concatenate([x, got[1], got[2], got[3]], axis=0)
    return received([x] * 4)


def summed(pieces):
    return sum(p.astype(jnp.float32) for p in pieces)


def scattered(pieces):
    total = summed(received(pieces)).astype(jnp.bfloat16)
    blocks = among_sixteen(total.reshape(16, -1, total.shape[-1]))
    return jnp.sum(blocks.astype(jnp.float32), axis=0)


def block_rows(relative):
    c = lax.axis_index("core")
    x, z, y = (lax.axis_index(a) for a in LATENT)
    k = np.arange(64)
    last, near, up = k // 16, (k // 4) % 4, k % 4
    if relative:
        bx = jnp.where(c == 0, near ^ x, last ^ x)
        by = jnp.where(c == 0, last ^ y, near ^ y)
        bz = up ^ z
    else:
        bx = jnp.where(c == 0, near, last ^ x)
        by = jnp.where(c == 0, last ^ y, near)
        bz = up
    return (BLOCK * (bx * 16 + bz * 4 + by)).astype(jnp.int32)


def relative_enc_kernel(rows, own, other, out, blocks):
    step = pl.program_id(0)
    for k in range(16):
        at = pl.ds(pl.multiple_of(rows[step * 16 + k], BLOCK), BLOCK)
        blocks[2 * k * BLOCK : (2 * k + 1) * BLOCK, :] = own[at, :]
        blocks[(2 * k + 1) * BLOCK : (2 * k + 2) * BLOCK, :] = other[at, :]
    out[0] = blocks[...].T


def relative_enc(rows, own, other):
    depth, n = own.shape
    whole = pl.BlockSpec((depth, n), lambda i: (0, 0))
    return pl.pallas_call(
        relative_enc_kernel,
        out_shape=jax.ShapeDtypeStruct((4, n, depth // 2), jnp.bfloat16),
        grid=(4,),
        in_specs=[SMEM, whole, whole],
        out_specs=pl.BlockSpec((1, n, depth // 2), lambda i: (i, 0, 0)),
        scratch_shapes=[pltpu.VMEM((depth // 2, n), jnp.bfloat16)],
        compiler_params=PARAMS,
        cost_estimate=pl.CostEstimate(flops=1 << 20, bytes_accessed=16 << 20, transcendentals=0),
    )(rows, own, other)


def relative_dec_kernel(rows, own, other, out, own_t, other_t):
    @pl.when(pl.program_id(0) == 0)
    def _():
        width = own.shape[1]
        for j in range(0, width, 512):
            own_t[j : j + 512, :] = own[:, j : j + 512].T
            other_t[j : j + 512, :] = other[:, j : j + 512].T

    step = pl.program_id(0)
    for k in range(16):
        at = pl.ds(pl.multiple_of(rows[step * 16 + k], BLOCK), BLOCK)
        out[0, 2 * k * BLOCK : (2 * k + 1) * BLOCK, :] = own_t[at, :]
        out[0, (2 * k + 1) * BLOCK : (2 * k + 2) * BLOCK, :] = other_t[at, :]


def relative_dec(rows, own, other):
    n, width = own.shape
    whole = pl.BlockSpec((n, width), lambda i: (0, 0))
    return pl.pallas_call(
        relative_dec_kernel,
        out_shape=jax.ShapeDtypeStruct((4, width // 2, n), jnp.bfloat16),
        grid=(4,),
        in_specs=[SMEM, whole, whole],
        out_specs=pl.BlockSpec((1, width // 2, n), lambda i: (i, 0, 0)),
        scratch_shapes=[pltpu.VMEM((width, n), jnp.bfloat16)] * 2,
        compiler_params=PARAMS,
        cost_estimate=pl.CostEstimate(flops=1 << 20, bytes_accessed=16 << 20, transcendentals=0),
    )(rows, own, other)


def turned_kernel(x, out):
    out[0] = x[0].T


def turned(x):
    m, n = x.shape[1:]
    return pl.pallas_call(
        turned_kernel,
        out_shape=jax.ShapeDtypeStruct((4, n, m), jnp.bfloat16),
        grid=(4,),
        in_specs=[pl.BlockSpec((1, m, n), lambda i: (i, 0, 0))],
        out_specs=pl.BlockSpec((1, n, m), lambda i: (i, 0, 0)),
        compiler_params=PARAMS,
        cost_estimate=pl.CostEstimate(flops=1 << 20, bytes_accessed=16 << 20, transcendentals=0),
    )(x)


def gathered_dot_kernel(w, p0, p1, p2, p3, out):
    terms = [
        jnp.dot(w[k], p[...], preferred_element_type=jnp.float32)
        for k, p in enumerate((p0, p1, p2, p3))
    ]
    out[...] = (terms[0] + terms[1] + terms[2] + terms[3]).astype(out.dtype)


def gathered_dot(w, pieces):
    _, n, depth = w.shape
    tokens = pieces[0].shape[1]
    return pl.pallas_call(
        gathered_dot_kernel,
        out_shape=jax.ShapeDtypeStruct((n, tokens), jnp.bfloat16),
        in_specs=[VMEM] * 5,
        out_specs=VMEM,
        compiler_params=SMALL,
        cost_estimate=pl.CostEstimate(
            flops=8 * n * depth * tokens, bytes_accessed=8 << 20, transcendentals=0
        ),
    )(w, *pieces)


def blocked_dot_kernel(w, part, part_b, bias, feat, *pieces):
    pre = part[...].astype(jnp.float32) + part_b[...].astype(jnp.float32) + bias[...]
    feat[...] = (jax.nn.softplus(4.0 * pre) / 4.0).astype(feat.dtype)
    for k in ORDER + (0,):
        pieces[k][...] = jnp.dot(w[k], feat[...], preferred_element_type=jnp.float32).astype(
            feat.dtype
        )


def blocked_dot(w, part, part_b, bias):
    _, width, n = w.shape
    tokens = part.shape[1]
    piece = jax.ShapeDtypeStruct((width, tokens), jnp.bfloat16)
    feat, *pieces = pl.pallas_call(
        blocked_dot_kernel,
        out_shape=(jax.ShapeDtypeStruct((n, tokens), jnp.bfloat16),) + (piece,) * 4,
        in_specs=[VMEM] * 4,
        out_specs=(VMEM,) * 5,
        compiler_params=SMALL,
        cost_estimate=pl.CostEstimate(
            flops=1 << 20, bytes_accessed=1 << 20, transcendentals=0
        ),
    )(w, part, part_b, bias)
    return feat, pieces


def placed_kernel(rows, *refs):
    pieces, (own, other) = refs[:-2], refs[-2:]
    tokens = pieces[0].shape[1]
    for k in range(64):
        at = pl.ds(pl.multiple_of(rows[k], BLOCK), BLOCK)
        src = (k % 16) * 2 * BLOCK
        for part in range(len(pieces) // 4):
            piece, to = pieces[part * 4 + k // 16], slice(part * tokens, (part + 1) * tokens)
            own[at, to] = piece[src : src + BLOCK, :]
            other[at, to] = piece[src + BLOCK : src + 2 * BLOCK, :]


def placed(rows, parts):
    depth, tokens = parts[0][0].shape
    whole = jax.ShapeDtypeStruct((2 * depth, len(parts) * tokens), jnp.bfloat16)
    return pl.pallas_call(
        placed_kernel,
        out_shape=(whole, whole),
        in_specs=[SMEM] + [VMEM] * (4 * len(parts)),
        out_specs=(VMEM,) * 2,
        compiler_params=SMALL,
        cost_estimate=pl.CostEstimate(flops=1 << 20, bytes_accessed=4 << 20, transcendentals=0),
    )(rows, *(p for part in parts for p in part))


def dot_nt(a, b):
    return lax.dot_general(a, b, (((1,), (1,)), ((), ())), preferred_element_type=jnp.float32)


def outer_dec_kernel(scale, feat, err, feat_b, err_b, out):
    left = jnp.concatenate([feat[...], feat_b[...]], axis=1)
    right = jnp.concatenate([err[...], err_b[...]], axis=1)
    out[...] = (scale * dot_nt(left, right)).astype(out.dtype)


def outer_dec(feat, err, feat_b, err_b, scale):
    m, tokens = feat.shape
    n = err.shape[0]
    tile = n // 4
    left = pl.BlockSpec((m, tokens), lambda i: (0, 0))
    right = pl.BlockSpec((tile, tokens), lambda i: (i, 0))
    return pl.pallas_call(
        functools.partial(outer_dec_kernel, scale),
        out_shape=jax.ShapeDtypeStruct((m, n), jnp.bfloat16),
        grid=(4,),
        in_specs=[left, right, left, right],
        out_specs=pl.BlockSpec((m, tile), lambda i: (0, i)),
        compiler_params=PARAMS,
        cost_estimate=pl.CostEstimate(
            flops=4 * m * n * tokens, bytes_accessed=5 << 20, transcendentals=0
        ),
    )(feat, err, feat_b, err_b)


def outer_enc_kernel(acts, grad, acts_b, grad_b, out, sums):
    left = jnp.concatenate([acts[...], acts_b[...]], axis=1)
    right = jnp.concatenate([grad[...], grad_b[...]], axis=1)
    out[...] = dot_nt(left, right).astype(out.dtype)

    @pl.when(pl.program_id(0) == 0)
    def _():
        ones = jnp.ones((8, grad.shape[1]), grad.dtype)
        sums[...] = (dot_nt(ones, grad[...]) + dot_nt(ones, grad_b[...]))[:1]


def outer_enc(acts, grad, acts_b, grad_b):
    m, tokens = acts.shape
    n = grad.shape[0]
    tile = m // 4
    rows = pl.BlockSpec((tile, tokens), lambda i: (i, 0))
    whole = pl.BlockSpec((n, tokens), lambda i: (0, 0))
    return pl.pallas_call(
        outer_enc_kernel,
        out_shape=(
            jax.ShapeDtypeStruct((m, n), jnp.bfloat16),
            jax.ShapeDtypeStruct((1, n), jnp.float32),
        ),
        grid=(4,),
        in_specs=[rows, whole, rows, whole],
        out_specs=(
            pl.BlockSpec((tile, n), lambda i: (i, 0)),
            pl.BlockSpec((1, n), lambda i: (0, 0)),
        ),
        compiler_params=PARAMS,
        cost_estimate=pl.CostEstimate(
            flops=40 * m * n * tokens, bytes_accessed=5 << 20, transcendentals=0
        ),
    )(acts, grad, acts_b, grad_b)


def body(acts, w_enc, b_enc, w_dec, b_dec):
    tokens_all = acts.shape[1]
    half = tokens_all // 2
    scale = tokens_all ** (-0.5)
    core = lax.axis_index("core")
    rows, acts_rows = block_rows(False), block_rows(True)

    local = acts[0].T
    swapped = other_core(local)
    start = jnp.concatenate(
        [lax.dynamic_slice_in_dim(a, core * half, half, 1) for a in (local, swapped)], axis=0
    )

    start, enc, dec, bias = lax.optimization_barrier((start, w_enc[0], w_dec[0], b_dec))
    enc_other, dec_other, bias_other = other_core(enc), other_core(dec), other_core(bias)
    enc_r = relative_enc(acts_rows, enc, enc_other)
    dec_r = relative_dec(rows, dec, dec_other)
    acts_p = gathered_by_permutes(start)

    part = gathered_dot(enc_r, acts_p)
    part, acts_p = lax.optimization_barrier((part, acts_p))
    part_b = other_layer(part)
    acts_own, acts_other = placed(acts_rows, [acts_p])
    part_b, acts_own, acts_other = lax.optimization_barrier((part_b, acts_own, acts_other))
    b_lanes = jnp.broadcast_to(b_enc[:, None], part.shape)
    feat, recon = blocked_dot(dec_r, part, part_b, b_lanes)
    recon = scattered(recon)
    recon, acts_b, feat_b = lax.optimization_barrier(
        (recon, other_core(acts_other), other_core(feat))
    )
    bias_both = jnp.concatenate([bias[0], bias_other[0]])[:, None]
    err = (recon + bias_both.astype(jnp.float32) - start.astype(jnp.float32)).astype(jnp.bfloat16)

    sums = jnp.sum(err.astype(jnp.float32), axis=1)
    width = sums.shape[0] // 2
    grad_bdec = scale * (sums[:width] + other_core(sums[width:]))
    err_p = gathered(err)
    err_p[0][2], dec_r = lax.optimization_barrier((err_p[0][2], dec_r))
    dec_rt = turned(dec_r)
    err_p[1], grad_bdec = lax.optimization_barrier((err_p[1], grad_bdec))
    term = [gathered_dot(dec_rt, pieces) for pieces in err_p]
    term_b = [other_layer(term[0]), None]
    term_b[0], term[1], err_p, feat = lax.optimization_barrier((term_b[0], term[1], err_p, feat))
    term_b[1] = other_layer(term[1])
    err_own, err_other = placed(rows, err_p)
    err_b = other_core(err_other)
    grad_dec = outer_dec(feat, err_own, feat_b, err_b, scale)
    term_b[1], grad_dec = lax.optimization_barrier((term_b[1], grad_dec))

    term, term_b = (jnp.concatenate(t, axis=1).astype(jnp.float32) for t in (term, term_b))
    pre = part.astype(jnp.float32) + part_b.astype(jnp.float32) + b_enc[:, None]
    grad_pre = (scale * (term + term_b) * jax.nn.sigmoid(4.0 * pre)).astype(jnp.bfloat16)
    grad_enc, grad_benc = outer_enc(acts_own, grad_pre, acts_b, other_core(grad_pre))
    grad_benc = grad_benc[0]
    return (grad_enc[None], grad_dec[None], grad_benc, grad_bdec[None])


def solution(mesh):
    finer = Mesh(mesh.devices.reshape(2, 2, 4, 4, 4), AXES)
    layer = ("z_lo", "core")
    return jax.shard_map(
        body,
        mesh=finer,
        in_specs=(
            P(layer, None, LATENT),
            P(layer, None, LATENT),
            P(LATENT),
            P(layer, LATENT, None),
            P(layer, LATENT),
        ),
        out_specs=(
            P(layer, None, LATENT),
            P(layer, LATENT, None),
            P(LATENT),
            P(layer, LATENT),
        ),
        check_vma=False,
    )
```

```python
import jax
import jax.numpy as jnp
import numpy as np
from jax import lax
from jax.experimental import pallas as pl
from jax.experimental.pallas import tpu as pltpu
from jax.sharding import Mesh
from jax.sharding import PartitionSpec as P

AXES = ("z_lo", "core", "x", "z_hi", "y")
LATENT = ("x", "z_hi", "y")
PLANE = ("core", "x", "y")
SPACE = ("core", "x", "z_hi", "y")
GROUPS = [
    [((c * 4 + (i if c == 0 else j)) * 4 + z) * 4 + (j if c == 0 else i) for i in range(4) for z in range(4)]
    for c in range(2)
    for j in range(4)
]
ORDER = (2, 1, 3)
BLOCK = 32

VMEM = pl.BlockSpec(memory_space=pltpu.VMEM)
SMEM = pl.BlockSpec(memory_space=pltpu.SMEM)
PARAMS = pltpu.CompilerParams(vmem_limit_bytes=16 * 1024 * 1024)
SMALL = pltpu.CompilerParams(vmem_limit_bytes=6 * 1024 * 1024)


def other_core(x):
    return lax.ppermute(x, "core", [(0, 1), (1, 0)])


def other_layer(x):
    return lax.ppermute(x, "z_lo", [(0, 1), (1, 0)])


def among_sixteen(x):
    return lax.all_to_all(x, SPACE, 0, 0, axis_index_groups=GROUPS, tiled=True)


def in_plane(x, k, x_core):
    pairs = []
    for c in range(2):
        for i in range(4):
            for j in range(4):
                a, b = (i ^ k, j) if c == x_core else (i, j ^ k)
                pairs.append((c * 16 + i * 4 + j, c * 16 + a * 4 + b))
    return lax.ppermute(x, PLANE, pairs)


def along_last(x, k):
    return in_plane(x, k, 1)


def received(pieces):
    got = {k: along_last(pieces[k], k) for k in ORDER}
    return [pieces[0], got[1], got[2], got[3]]


def along_z(x, k):
    return lax.ppermute(x, "z_hi", [(i, i ^ k) for i in range(4)])


def along_first(x, k):
    return in_plane(x, k, 0)


def in_two(x):
    return [received([g] * 4) for g in jnp.split(x, 2, axis=1)]


def gathered(x):
    x = among_sixteen(jnp.broadcast_to(x[None], (16, *x.shape)))
    return in_two(x.reshape(-1, x.shape[-1]))


def gathered_by_permutes(x):
    for send in (along_z, along_first):
        got = {k: send(x, k) for k in ORDER}
        x = jnp.concatenate([x, got[1], got[2], got[3]], axis=0)
    return received([x] * 4)


def summed(pieces):
    return sum(p.astype(jnp.float32) for p in pieces)


def scattered(pieces, beside):
    total = summed(received(pieces)).astype(jnp.bfloat16)
    total, beside = lax.optimization_barrier((total, beside))
    blocks = among_sixteen(total.reshape(16, -1, total.shape[-1]))
    return jnp.sum(blocks.astype(jnp.float32), axis=0), beside


def block_rows(relative):
    c = lax.axis_index("core")
    x, z, y = (lax.axis_index(a) for a in LATENT)
    k = np.arange(64)
    last, near, up = k // 16, (k // 4) % 4, k % 4
    if relative:
        bx = jnp.where(c == 0, near ^ x, last ^ x)
        by = jnp.where(c == 0, last ^ y, near ^ y)
        bz = up ^ z
    else:
        bx = jnp.where(c == 0, near, last ^ x)
        by = jnp.where(c == 0, last ^ y, near)
        bz = up
    return (BLOCK * (bx * 16 + bz * 4 + by)).astype(jnp.int32)


def relative_enc_kernel(rows, own, other, out, blocks):
    step = pl.program_id(0)
    for k in range(16):
        at = pl.ds(pl.multiple_of(rows[step * 16 + k], BLOCK), BLOCK)
        blocks[2 * k * BLOCK : (2 * k + 1) * BLOCK, :] = own[at, :]
        blocks[(2 * k + 1) * BLOCK : (2 * k + 2) * BLOCK, :] = other[at, :]
    out[0] = blocks[...].T


def relative_enc(rows, own, other):
    depth, n = own.shape
    whole = pl.BlockSpec((depth, n), lambda i: (0, 0))
    return pl.pallas_call(
        relative_enc_kernel,
        out_shape=jax.ShapeDtypeStruct((4, n, depth // 2), jnp.bfloat16),
        grid=(4,),
        in_specs=[SMEM, whole, whole],
        out_specs=pl.BlockSpec((1, n, depth // 2), lambda i: (i, 0, 0)),
        scratch_shapes=[pltpu.VMEM((depth // 2, n), jnp.bfloat16)],
        compiler_params=PARAMS,
        cost_estimate=pl.CostEstimate(flops=1 << 20, bytes_accessed=16 << 20, transcendentals=0),
    )(rows, own, other)


def relative_dec_kernel(rows, own, other, out, own_t, other_t):
    @pl.when(pl.program_id(0) == 0)
    def _():
        width = own.shape[1]
        for j in range(0, width, 512):
            own_t[j : j + 512, :] = own[:, j : j + 512].T
            other_t[j : j + 512, :] = other[:, j : j + 512].T

    step = pl.program_id(0)
    for k in range(16):
        at = pl.ds(pl.multiple_of(rows[step * 16 + k], BLOCK), BLOCK)
        out[0, 2 * k * BLOCK : (2 * k + 1) * BLOCK, :] = own_t[at, :]
        out[0, (2 * k + 1) * BLOCK : (2 * k + 2) * BLOCK, :] = other_t[at, :]


def relative_dec(rows, own, other):
    n, width = own.shape
    whole = pl.BlockSpec((n, width), lambda i: (0, 0))
    return pl.pallas_call(
        relative_dec_kernel,
        out_shape=jax.ShapeDtypeStruct((4, width // 2, n), jnp.bfloat16),
        grid=(4,),
        in_specs=[SMEM, whole, whole],
        out_specs=pl.BlockSpec((1, width // 2, n), lambda i: (i, 0, 0)),
        scratch_shapes=[pltpu.VMEM((width, n), jnp.bfloat16)] * 2,
        compiler_params=PARAMS,
        cost_estimate=pl.CostEstimate(flops=1 << 20, bytes_accessed=16 << 20, transcendentals=0),
    )(rows, own, other)


def turned_kernel(x, out):
    out[0] = x[0].T


def turned(x):
    m, n = x.shape[1:]
    return pl.pallas_call(
        turned_kernel,
        out_shape=jax.ShapeDtypeStruct((4, n, m), jnp.bfloat16),
        grid=(4,),
        in_specs=[pl.BlockSpec((1, m, n), lambda i: (i, 0, 0))],
        out_specs=pl.BlockSpec((1, n, m), lambda i: (i, 0, 0)),
        compiler_params=PARAMS,
        cost_estimate=pl.CostEstimate(flops=1 << 20, bytes_accessed=16 << 20, transcendentals=0),
    )(x)


def gathered_dot_kernel(w, p0, p1, p2, p3, out):
    terms = [
        jnp.dot(w[k], p[...], preferred_element_type=jnp.float32)
        for k, p in enumerate((p0, p1, p2, p3))
    ]
    out[...] = (terms[0] + terms[1] + terms[2] + terms[3]).astype(out.dtype)


def gathered_dot(w, pieces):
    _, n, depth = w.shape
    tokens = pieces[0].shape[1]
    return pl.pallas_call(
        gathered_dot_kernel,
        out_shape=jax.ShapeDtypeStruct((n, tokens), jnp.bfloat16),
        in_specs=[VMEM] * 5,
        out_specs=VMEM,
        compiler_params=SMALL,
        cost_estimate=pl.CostEstimate(
            flops=8 * n * depth * tokens, bytes_accessed=8 << 20, transcendentals=0
        ),
    )(w, *pieces)


def blocked_dot_kernel(w, part, part_b, bias, feat, *pieces):
    pre = part[...].astype(jnp.float32) + part_b[...].astype(jnp.float32) + bias[...]
    feat[...] = (jax.nn.softplus(4.0 * pre) / 4.0).astype(feat.dtype)
    for k in ORDER + (0,):
        pieces[k][...] = jnp.dot(w[k], feat[...], preferred_element_type=jnp.float32).astype(
            feat.dtype
        )


def blocked_dot(w, part, part_b, bias):
    _, width, n = w.shape
    tokens = part.shape[1]
    piece = jax.ShapeDtypeStruct((width, tokens), jnp.bfloat16)
    feat, *pieces = pl.pallas_call(
        blocked_dot_kernel,
        out_shape=(jax.ShapeDtypeStruct((n, tokens), jnp.bfloat16),) + (piece,) * 4,
        in_specs=[VMEM] * 4,
        out_specs=(VMEM,) * 5,
        compiler_params=SMALL,
        cost_estimate=pl.CostEstimate(
            flops=1 << 20, bytes_accessed=1 << 20, transcendentals=0
        ),
    )(w, part, part_b, bias)
    return feat, pieces


def placed_kernel(rows, *refs):
    pieces, (own, other) = refs[:-2], refs[-2:]
    tokens = pieces[0].shape[1]
    for k in range(64):
        at = pl.ds(pl.multiple_of(rows[k], BLOCK), BLOCK)
        src = (k % 16) * 2 * BLOCK
        for part in range(len(pieces) // 4):
            piece, to = pieces[part * 4 + k // 16], slice(part * tokens, (part + 1) * tokens)
            own[at, to] = piece[src : src + BLOCK, :]
            other[at, to] = piece[src + BLOCK : src + 2 * BLOCK, :]


def placed(rows, parts):
    depth, tokens = parts[0][0].shape
    whole = jax.ShapeDtypeStruct((2 * depth, len(parts) * tokens), jnp.bfloat16)
    return pl.pallas_call(
        placed_kernel,
        out_shape=(whole, whole),
        in_specs=[SMEM] + [VMEM] * (4 * len(parts)),
        out_specs=(VMEM,) * 2,
        compiler_params=SMALL,
        cost_estimate=pl.CostEstimate(flops=1 << 20, bytes_accessed=4 << 20, transcendentals=0),
    )(rows, *(p for part in parts for p in part))


def dot_nt(a, b):
    return lax.dot_general(a, b, (((1,), (1,)), ((), ())), preferred_element_type=jnp.float32)


def outer_dec(feat, err, feat_b, err_b, scale):
    left, right = jnp.concatenate([feat, feat_b], axis=1), jnp.concatenate([err, err_b], axis=1)
    return (scale * dot_nt(left, right)).astype(jnp.bfloat16)


def outer_enc_kernel(acts, grad, acts_b, grad_b, out, sums):
    left = jnp.concatenate([acts[...], acts_b[...]], axis=1)
    right = jnp.concatenate([grad[...], grad_b[...]], axis=1)
    out[...] = dot_nt(left, right).astype(out.dtype)

    @pl.when(pl.program_id(0) == 0)
    def _():
        ones = jnp.ones((8, grad.shape[1]), grad.dtype)
        sums[...] = (dot_nt(ones, grad[...]) + dot_nt(ones, grad_b[...]))[:1]


def outer_enc(acts, grad, acts_b, grad_b):
    m, tokens = acts.shape
    n = grad.shape[0]
    tile = m // 2
    rows = pl.BlockSpec((tile, tokens), lambda i: (i, 0))
    whole = pl.BlockSpec((n, tokens), lambda i: (0, 0))
    return pl.pallas_call(
        outer_enc_kernel,
        out_shape=(
            jax.ShapeDtypeStruct((m, n), jnp.bfloat16),
            jax.ShapeDtypeStruct((1, n), jnp.float32),
        ),
        grid=(2,),
        in_specs=[rows, whole, rows, whole],
        out_specs=(
            pl.BlockSpec((tile, n), lambda i: (i, 0)),
            pl.BlockSpec((1, n), lambda i: (0, 0)),
        ),
        compiler_params=PARAMS,
        cost_estimate=pl.CostEstimate(
            flops=40 * m * n * tokens, bytes_accessed=5 << 20, transcendentals=0
        ),
    )(acts, grad, acts_b, grad_b)


def body(acts, w_enc, b_enc, w_dec, b_dec):
    tokens_all = acts.shape[1]
    half = tokens_all // 2
    scale = tokens_all ** (-0.5)
    core = lax.axis_index("core")
    rows, acts_rows = block_rows(False), block_rows(True)

    local = acts[0].T
    swapped = other_core(local)
    start = jnp.concatenate(
        [lax.dynamic_slice_in_dim(a, core * half, half, 1) for a in (local, swapped)], axis=0
    )

    start, enc, dec, bias = lax.optimization_barrier((start, w_enc[0], w_dec[0], b_dec))
    enc_other, dec_other, bias_other = other_core(enc), other_core(dec), other_core(bias)
    enc_r = relative_enc(acts_rows, enc, enc_other)
    dec_r = relative_dec(rows, dec, dec_other)
    acts_p = gathered_by_permutes(start)

    part = gathered_dot(enc_r, acts_p)
    part, acts_p = lax.optimization_barrier((part, acts_p))
    part_b = other_layer(part)
    acts_own, acts_other = placed(acts_rows, [acts_p])
    part_b, acts_own, acts_other = lax.optimization_barrier((part_b, acts_own, acts_other))
    b_lanes = jnp.broadcast_to(b_enc[:, None], part.shape)
    feat, recon = blocked_dot(dec_r, part, part_b, b_lanes)
    recon, dec_rt = scattered(recon, turned(dec_r))
    recon, acts_b, feat_b = lax.optimization_barrier(
        (recon, other_core(acts_other), other_core(feat))
    )
    bias_both = jnp.concatenate([bias[0], bias_other[0]])[:, None]
    err = (recon + bias_both.astype(jnp.float32) - start.astype(jnp.float32)).astype(jnp.bfloat16)

    sums = jnp.sum(err.astype(jnp.float32), axis=1)
    width = sums.shape[0] // 2
    grad_bdec = scale * (sums[:width] + other_core(sums[width:]))
    err_p = gathered(err)
    err_p[1], grad_bdec = lax.optimization_barrier((err_p[1], grad_bdec))
    term = [gathered_dot(dec_rt, pieces) for pieces in err_p]
    term_b = [other_layer(term[0]), None]
    term_b[0], term[1], err_p, feat = lax.optimization_barrier((term_b[0], term[1], err_p, feat))
    term_b[1] = other_layer(term[1])
    err_own, err_other = placed(rows, err_p)
    err_b = other_core(err_other)
    grad_dec = outer_dec(feat, err_own, feat_b, err_b, scale)
    term_b[1], grad_dec = lax.optimization_barrier((term_b[1], grad_dec))

    term, term_b = (jnp.concatenate(t, axis=1).astype(jnp.float32) for t in (term, term_b))
    pre = part.astype(jnp.float32) + part_b.astype(jnp.float32) + b_enc[:, None]
    grad_pre = (scale * (term + term_b) * jax.nn.sigmoid(4.0 * pre)).astype(jnp.bfloat16)
    grad_enc, grad_benc = outer_enc(acts_own, grad_pre, acts_b, other_core(grad_pre))
    grad_benc = grad_benc[0]
    return (grad_enc[None], grad_dec[None], grad_benc, grad_bdec[None])


def solution(mesh):
    finer = Mesh(mesh.devices.reshape(2, 2, 4, 4, 4), AXES)
    layer = ("z_lo", "core")
    return jax.shard_map(
        body,
        mesh=finer,
        in_specs=(
            P(layer, None, LATENT),
            P(layer, None, LATENT),
            P(LATENT),
            P(layer, LATENT, None),
            P(layer, LATENT),
        ),
        out_specs=(
            P(layer, None, LATENT),
            P(layer, LATENT, None),
            P(LATENT),
            P(layer, LATENT),
        ),
        check_vma=False,
    )
```

```python
import functools

import jax
import jax.numpy as jnp
import numpy as np
from jax import lax
from jax.experimental import pallas as pl
from jax.experimental.pallas import tpu as pltpu
from jax.sharding import Mesh
from jax.sharding import PartitionSpec as P

AXES = ("z_lo", "core", "x", "z_hi", "y")
LATENT = ("x", "z_hi", "y")
PLANE = ("core", "x", "y")
SPACE = ("core", "x", "z_hi", "y")
GROUPS = [
    [((c * 4 + (i if c == 0 else j)) * 4 + z) * 4 + (j if c == 0 else i) for i in range(4) for z in range(4)]
    for c in range(2)
    for j in range(4)
]
ORDER = (2, 1, 3)
BLOCK = 32

VMEM = pl.BlockSpec(memory_space=pltpu.VMEM)
SMEM = pl.BlockSpec(memory_space=pltpu.SMEM)
PARAMS = pltpu.CompilerParams(vmem_limit_bytes=16 * 1024 * 1024)
SMALL = pltpu.CompilerParams(vmem_limit_bytes=6 * 1024 * 1024)


def other_core(x):
    return lax.ppermute(x, "core", [(0, 1), (1, 0)])


def other_layer(x):
    return lax.ppermute(x, "z_lo", [(0, 1), (1, 0)])


def among_sixteen(x):
    return lax.all_to_all(x, SPACE, 0, 0, axis_index_groups=GROUPS, tiled=True)


def in_plane(x, k, x_core):
    pairs = []
    for c in range(2):
        for i in range(4):
            for j in range(4):
                a, b = (i ^ k, j) if c == x_core else (i, j ^ k)
                pairs.append((c * 16 + i * 4 + j, c * 16 + a * 4 + b))
    return lax.ppermute(x, PLANE, pairs)


def along_last(x, k):
    return in_plane(x, k, 1)


def received(pieces):
    got = {k: along_last(pieces[k], k) for k in ORDER}
    return [pieces[0], got[1], got[2], got[3]]


def along_z(x, k):
    return lax.ppermute(x, "z_hi", [(i, i ^ k) for i in range(4)])


def along_first(x, k):
    return in_plane(x, k, 0)


def in_two(x):
    return [received([g] * 4) for g in jnp.split(x, 2, axis=1)]


def gathered(x):
    x = among_sixteen(jnp.broadcast_to(x[None], (16, *x.shape)))
    return in_two(x.reshape(-1, x.shape[-1]))


def gathered_by_permutes(x):
    for send in (along_z, along_first):
        got = {k: send(x, k) for k in ORDER}
        x = jnp.concatenate([x, got[1], got[2], got[3]], axis=0)
    return received([x] * 4)


def summed(pieces):
    return sum(p.astype(jnp.float32) for p in pieces)


def scattered(pieces, beside):
    total = summed(received(pieces)).astype(jnp.bfloat16)
    total, beside = lax.optimization_barrier((total, beside))
    blocks = among_sixteen(total.reshape(16, -1, total.shape[-1]))
    return jnp.sum(blocks.astype(jnp.float32), axis=0), beside


def block_rows(relative):
    c = lax.axis_index("core")
    x, z, y = (lax.axis_index(a) for a in LATENT)
    k = np.arange(64)
    last, near, up = k // 16, (k // 4) % 4, k % 4
    if relative:
        bx = jnp.where(c == 0, near ^ x, last ^ x)
        by = jnp.where(c == 0, last ^ y, near ^ y)
        bz = up ^ z
    else:
        bx = jnp.where(c == 0, near, last ^ x)
        by = jnp.where(c == 0, last ^ y, near)
        bz = up
    return (BLOCK * (bx * 16 + bz * 4 + by)).astype(jnp.int32)


def relative_enc_kernel(rows, own, other, out, blocks):
    step = pl.program_id(0)
    for k in range(16):
        at = pl.ds(pl.multiple_of(rows[step * 16 + k], BLOCK), BLOCK)
        blocks[2 * k * BLOCK : (2 * k + 1) * BLOCK, :] = own[at, :]
        blocks[(2 * k + 1) * BLOCK : (2 * k + 2) * BLOCK, :] = other[at, :]
    out[0] = blocks[...].T


def relative_enc(rows, own, other):
    depth, n = own.shape
    whole = pl.BlockSpec((depth, n), lambda i: (0, 0))
    return pl.pallas_call(
        relative_enc_kernel,
        out_shape=jax.ShapeDtypeStruct((4, n, depth // 2), jnp.bfloat16),
        grid=(4,),
        in_specs=[SMEM, whole, whole],
        out_specs=pl.BlockSpec((1, n, depth // 2), lambda i: (i, 0, 0)),
        scratch_shapes=[pltpu.VMEM((depth // 2, n), jnp.bfloat16)],
        compiler_params=PARAMS,
        cost_estimate=pl.CostEstimate(flops=1 << 20, bytes_accessed=16 << 20, transcendentals=0),
    )(rows, own, other)


def relative_dec_kernel(rows, own, other, out, own_t, other_t):
    @pl.when(pl.program_id(0) == 0)
    def _():
        width = own.shape[1]
        for j in range(0, width, 512):
            own_t[j : j + 512, :] = own[:, j : j + 512].T
            other_t[j : j + 512, :] = other[:, j : j + 512].T

    step = pl.program_id(0)
    for k in range(16):
        at = pl.ds(pl.multiple_of(rows[step * 16 + k], BLOCK), BLOCK)
        out[0, 2 * k * BLOCK : (2 * k + 1) * BLOCK, :] = own_t[at, :]
        out[0, (2 * k + 1) * BLOCK : (2 * k + 2) * BLOCK, :] = other_t[at, :]


def relative_dec(rows, own, other):
    n, width = own.shape
    whole = pl.BlockSpec((n, width), lambda i: (0, 0))
    return pl.pallas_call(
        relative_dec_kernel,
        out_shape=jax.ShapeDtypeStruct((4, width // 2, n), jnp.bfloat16),
        grid=(4,),
        in_specs=[SMEM, whole, whole],
        out_specs=pl.BlockSpec((1, width // 2, n), lambda i: (i, 0, 0)),
        scratch_shapes=[pltpu.VMEM((width, n), jnp.bfloat16)] * 2,
        compiler_params=PARAMS,
        cost_estimate=pl.CostEstimate(flops=1 << 20, bytes_accessed=16 << 20, transcendentals=0),
    )(rows, own, other)


def turned_kernel(x, out):
    out[0] = x[0].T


def turned(x):
    m, n = x.shape[1:]
    return pl.pallas_call(
        turned_kernel,
        out_shape=jax.ShapeDtypeStruct((4, n, m), jnp.bfloat16),
        grid=(4,),
        in_specs=[pl.BlockSpec((1, m, n), lambda i: (i, 0, 0))],
        out_specs=pl.BlockSpec((1, n, m), lambda i: (i, 0, 0)),
        compiler_params=PARAMS,
        cost_estimate=pl.CostEstimate(flops=1 << 20, bytes_accessed=16 << 20, transcendentals=0),
    )(x)


def gathered_dot_kernel(w, p0, p1, p2, p3, out):
    terms = [
        jnp.dot(w[k], p[...], preferred_element_type=jnp.float32)
        for k, p in enumerate((p0, p1, p2, p3))
    ]
    out[...] = (terms[0] + terms[1] + terms[2] + terms[3]).astype(out.dtype)


def gathered_dot(w, pieces):
    _, n, depth = w.shape
    tokens = pieces[0].shape[1]
    return pl.pallas_call(
        gathered_dot_kernel,
        out_shape=jax.ShapeDtypeStruct((n, tokens), jnp.bfloat16),
        in_specs=[VMEM] * 5,
        out_specs=VMEM,
        compiler_params=SMALL,
        cost_estimate=pl.CostEstimate(
            flops=8 * n * depth * tokens, bytes_accessed=8 << 20, transcendentals=0
        ),
    )(w, *pieces)


def blocked_dot_kernel(w, part, part_b, bias, feat, *pieces):
    pre = part[...].astype(jnp.float32) + part_b[...].astype(jnp.float32) + bias[...]
    feat[...] = (jax.nn.softplus(4.0 * pre) / 4.0).astype(feat.dtype)
    for k in ORDER + (0,):
        pieces[k][...] = jnp.dot(w[k], feat[...], preferred_element_type=jnp.float32).astype(
            feat.dtype
        )


def blocked_dot(w, part, part_b, bias):
    _, width, n = w.shape
    tokens = part.shape[1]
    piece = jax.ShapeDtypeStruct((width, tokens), jnp.bfloat16)
    feat, *pieces = pl.pallas_call(
        blocked_dot_kernel,
        out_shape=(jax.ShapeDtypeStruct((n, tokens), jnp.bfloat16),) + (piece,) * 4,
        in_specs=[VMEM] * 4,
        out_specs=(VMEM,) * 5,
        compiler_params=SMALL,
        cost_estimate=pl.CostEstimate(
            flops=1 << 20, bytes_accessed=1 << 20, transcendentals=0
        ),
    )(w, part, part_b, bias)
    return feat, pieces


def placed_kernel(rows, *refs):
    pieces, (own, other) = refs[:-2], refs[-2:]
    tokens = pieces[0].shape[1]
    for k in range(64):
        at = pl.ds(pl.multiple_of(rows[k], BLOCK), BLOCK)
        src = (k % 16) * 2 * BLOCK
        for part in range(len(pieces) // 4):
            piece, to = pieces[part * 4 + k // 16], slice(part * tokens, (part + 1) * tokens)
            own[at, to] = piece[src : src + BLOCK, :]
            other[at, to] = piece[src + BLOCK : src + 2 * BLOCK, :]


def placed(rows, parts):
    depth, tokens = parts[0][0].shape
    whole = jax.ShapeDtypeStruct((2 * depth, len(parts) * tokens), jnp.bfloat16)
    return pl.pallas_call(
        placed_kernel,
        out_shape=(whole, whole),
        in_specs=[SMEM] + [VMEM] * (4 * len(parts)),
        out_specs=(VMEM,) * 2,
        compiler_params=SMALL,
        cost_estimate=pl.CostEstimate(flops=1 << 20, bytes_accessed=4 << 20, transcendentals=0),
    )(rows, *(p for part in parts for p in part))


def dot_nt(a, b):
    return lax.dot_general(a, b, (((1,), (1,)), ((), ())), preferred_element_type=jnp.float32)


def outer_dec_kernel(scale, feat, err, feat_b, err_b, out):
    left = jnp.concatenate([feat[...], feat_b[...]], axis=1)
    right = jnp.concatenate([err[...], err_b[...]], axis=1)
    out[...] = (scale * dot_nt(left, right)).astype(out.dtype)


def outer_dec(feat, err, feat_b, err_b, scale):
    m, tokens = feat.shape
    n = err.shape[0]
    tile = n // 2
    left = pl.BlockSpec((m, tokens), lambda i: (0, 0))
    right = pl.BlockSpec((tile, tokens), lambda i: (i, 0))
    return pl.pallas_call(
        functools.partial(outer_dec_kernel, scale),
        out_shape=jax.ShapeDtypeStruct((m, n), jnp.bfloat16),
        grid=(2,),
        in_specs=[left, right, left, right],
        out_specs=pl.BlockSpec((m, tile), lambda i: (0, i)),
        compiler_params=PARAMS,
        cost_estimate=pl.CostEstimate(
            flops=4 * m * n * tokens, bytes_accessed=5 << 20, transcendentals=0
        ),
    )(feat, err, feat_b, err_b)


def outer_enc_kernel(acts, grad, acts_b, grad_b, out, sums):
    left = jnp.concatenate([acts[...], acts_b[...]], axis=1)
    right = jnp.concatenate([grad[...], grad_b[...]], axis=1)
    out[...] = dot_nt(left, right).astype(out.dtype)

    @pl.when(pl.program_id(0) == 0)
    def _():
        ones = jnp.ones((8, grad.shape[1]), grad.dtype)
        sums[...] = (dot_nt(ones, grad[...]) + dot_nt(ones, grad_b[...]))[:1]


def outer_enc(acts, grad, acts_b, grad_b):
    m, tokens = acts.shape
    n = grad.shape[0]
    tile = m // 2
    rows = pl.BlockSpec((tile, tokens), lambda i: (i, 0))
    whole = pl.BlockSpec((n, tokens), lambda i: (0, 0))
    return pl.pallas_call(
        outer_enc_kernel,
        out_shape=(
            jax.ShapeDtypeStruct((m, n), jnp.bfloat16),
            jax.ShapeDtypeStruct((1, n), jnp.float32),
        ),
        grid=(2,),
        in_specs=[rows, whole, rows, whole],
        out_specs=(
            pl.BlockSpec((tile, n), lambda i: (i, 0)),
            pl.BlockSpec((1, n), lambda i: (0, 0)),
        ),
        compiler_params=PARAMS,
        cost_estimate=pl.CostEstimate(
            flops=40 * m * n * tokens, bytes_accessed=5 << 20, transcendentals=0
        ),
    )(acts, grad, acts_b, grad_b)


def body(acts, w_enc, b_enc, w_dec, b_dec):
    tokens_all = acts.shape[1]
    half = tokens_all // 2
    scale = tokens_all ** (-0.5)
    core = lax.axis_index("core")
    rows, acts_rows = block_rows(False), block_rows(True)

    local = acts[0].T
    swapped = other_core(local)
    start = jnp.concatenate(
        [lax.dynamic_slice_in_dim(a, core * half, half, 1) for a in (local, swapped)], axis=0
    )

    start, enc, dec, bias = lax.optimization_barrier((start, w_enc[0], w_dec[0], b_dec))
    enc_other, dec_other, bias_other = other_core(enc), other_core(dec), other_core(bias)
    enc_r = relative_enc(acts_rows, enc, enc_other)
    dec_r = relative_dec(rows, dec, dec_other)
    acts_p = gathered_by_permutes(start)

    part = gathered_dot(enc_r, acts_p)
    part, acts_p = lax.optimization_barrier((part, acts_p))
    part_b = other_layer(part)
    acts_own, acts_other = placed(acts_rows, [acts_p])
    part_b, acts_own, acts_other = lax.optimization_barrier((part_b, acts_own, acts_other))
    b_lanes = jnp.broadcast_to(b_enc[:, None], part.shape)
    feat, recon = blocked_dot(dec_r, part, part_b, b_lanes)
    recon, dec_rt = scattered(recon, turned(dec_r))
    recon, acts_b, feat_b = lax.optimization_barrier(
        (recon, other_core(acts_other), other_core(feat))
    )
    bias_both = jnp.concatenate([bias[0], bias_other[0]])[:, None]
    err = (recon + bias_both.astype(jnp.float32) - start.astype(jnp.float32)).astype(jnp.bfloat16)

    sums = jnp.sum(err.astype(jnp.float32), axis=1)
    width = sums.shape[0] // 2
    grad_bdec = scale * (sums[:width] + other_core(sums[width:]))
    err_p = gathered(err)
    err_p[1], grad_bdec = lax.optimization_barrier((err_p[1], grad_bdec))
    term = [gathered_dot(dec_rt, pieces) for pieces in err_p]
    term_b = [other_layer(t) for t in term]
    term[1], err_p = lax.optimization_barrier((term[1], err_p))
    err_own, err_other = placed(rows, err_p)
    term_b[1], err_own, err_other = lax.optimization_barrier((term_b[1], err_own, err_other))
    err_b = other_core(err_other)
    grad_dec = outer_dec(feat, err_own, feat_b, err_b, scale)

    term, term_b = (jnp.concatenate(t, axis=1).astype(jnp.float32) for t in (term, term_b))
    pre = part.astype(jnp.float32) + part_b.astype(jnp.float32) + b_enc[:, None]
    grad_pre = (scale * (term + term_b) * jax.nn.sigmoid(4.0 * pre)).astype(jnp.bfloat16)
    grad_enc, grad_benc = outer_enc(acts_own, grad_pre, acts_b, other_core(grad_pre))
    grad_benc = grad_benc[0]
    return (grad_enc[None], grad_dec[None], grad_benc, grad_bdec[None])


def solution(mesh):
    finer = Mesh(mesh.devices.reshape(2, 2, 4, 4, 4), AXES)
    layer = ("z_lo", "core")
    return jax.shard_map(
        body,
        mesh=finer,
        in_specs=(
            P(layer, None, LATENT),
            P(layer, None, LATENT),
            P(LATENT),
            P(layer, LATENT, None),
            P(layer, LATENT),
        ),
        out_specs=(
            P(layer, None, LATENT),
            P(layer, LATENT, None),
            P(LATENT),
            P(layer, LATENT),
        ),
        check_vma=False,
    )
```
